256 devices in a mesh: seq: 32 (over y, z), head: 8 (over x, core).
Axes of the slice: x: 4, y: 4, z: 8, core: 2. Of those that a mesh axis runs over, the one named last changes fastest.
Arguments:
- teacher_query: bfloat16 [4096, 4096], P('seq', 'head'), may hold values from -20 to 20
- teacher_key: bfloat16 [4096, 4096], P('seq', 'head'), may hold values from -20 to 20
- student_query: bfloat16 [4096, 2048], P('seq', 'head'), may hold values from -20 to 20
- student_key: bfloat16 [4096, 2048], P('seq', 'head'), may hold values from -20 to 20
- doc_ids: int32 [4096], P('seq'), may hold values from 0 to 15, never falling along the last dimension, each value on 1 to 3072 neighbouring positions
Outputs:
- kl_loss: float32 [], replicated
- grad_query: bfloat16 [4096, 2048], P('seq', 'head')
- grad_key: bfloat16 [4096, 2048], P('seq', 'head')
The draws below stay inside these ranges and needn't reach their ends.
Inputs may be any that keep to these rules, and one draw needn't show every extreme that they name: `doc_ids`: ids never fall along the positions; every document is a run of at most 3072 positions and one has exactly 3072.
All inputs are finite; a program needn't handle non-finite values.
Results may differ from the reference program's by a relative error of at most 0.009.
Values may be sent and summed in bfloat16 or wider, within the bound.
No kernel may reach another device: no remote copies, remote signals or barrier semaphores. Data moves between devices by JAX's collectives and lax.ppermute only.
A program may use at most 64 MiB of HBM per device.

```python
import math
import jax
import jax.numpy as jnp
import numpy as np
from jax import lax

HDIM = 128
TDIM = 256
RHEADS = 16
SEGS = 16
TOKENS = 4096
LONGEST = 3072


def drawn_rows(key, columns):
    values = 0.8 * jax.random.normal(key, (TOKENS, columns), jnp.float32)
    return jnp.clip(values, -20.0, 20.0).astype(jnp.bfloat16)


def draw_teacher_query(key, part):
    key = jax.random.fold_in(key, 11)
    return drawn_rows(key, RHEADS * TDIM)


def draw_teacher_key(key, part):
    key = jax.random.fold_in(key, 12)
    return drawn_rows(key, RHEADS * TDIM)


def draw_student_query(key, part):
    key = jax.random.fold_in(key, 13)
    return drawn_rows(key, RHEADS * HDIM)


def draw_student_key(key, part):
    key = jax.random.fold_in(key, 14)
    return drawn_rows(key, RHEADS * HDIM)


def profile(count, total, most, slope):
    portions = [(1 << 20) // math.isqrt(rank ** slope) + 1 for rank in range(2, count + 1)]
    rest, counts = total - most - (count - 1), [1] * (count - 1)
    while rest > 0:
        free = [i for i in range(count - 1) if counts[i] < most]
        pool, remaining = sum([portions[i] for i in free]), rest
        for i in free:
            addition = min(most - counts[i], max(1, remaining * portions[i] // pool), rest)
            counts[i] = counts[i] + addition
            rest = rest - addition
    return np.array([most] + counts)


def ragged(stream_key, number_of, total, limit, slope):
    if number_of == 2:
        one = jax.random.randint(stream_key, (), max(1, total - limit), min(limit, total - 1) + 1)
        return jnp.stack([one, total - one])
    tallies = jnp.asarray(profile(number_of, total, limit, slope), jnp.int32)
    couples = (number_of - 1) // 2
    source_of, taker = tallies[1:1 + 2 * couples:2], tallies[2:2 + 2 * couples:2]
    room = jnp.minimum(source_of - 1, limit - taker)
    passed = jax.random.randint(jax.random.fold_in(stream_key, 1), (couples,), 0, 1 << 20) % (room + 1)
    tallies = tallies.at[1:1 + 2 * couples:2].set(source_of - passed).at[2:2 + 2 * couples:2].set(taker + passed)
    return tallies[jax.random.permutation(jax.random.fold_in(stream_key, 2), number_of)]


def setup_inputs(seed: int = 0) -> dict:
    key_of = jax.random.split(jax.random.key(seed), 6)
    return {
        "teacher_query": draw_teacher_query(jax.random.fold_in(key_of[5], 71), 0),
        "teacher_key": draw_teacher_key(jax.random.fold_in(key_of[5], 71), 0),
        "student_query": draw_student_query(jax.random.fold_in(key_of[5], 71), 0),
        "student_key": draw_student_key(jax.random.fold_in(key_of[5], 71), 0),
        "doc_ids": jnp.searchsorted(jnp.cumsum(ragged(key_of[4], SEGS, TOKENS, LONGEST, 2)), jnp.arange(TOKENS), side="right").astype(jnp.int32),
    }


NEG = -1e+30

def one_head(teach_rows, pupil_rows, doc_ids):
    length = teach_rows.shape[0]
    positions = jnp.arange(length, dtype=jnp.int32)
    visible = (doc_ids[:, None] == doc_ids[None, :]) & (positions[None, :] <= positions[:, None])
    teach_factor = 1.0 / math.sqrt(TDIM)
    pupil_factor = 1.0 / math.sqrt(HDIM)
    teacher_score = jnp.dot(teach_rows, teach_rows.T, preferred_element_type=jnp.float32) * teach_factor
    student_score = jnp.dot(pupil_rows, pupil_rows.T, preferred_element_type=jnp.float32) * pupil_factor
    lse_t = jax.nn.logsumexp(jnp.where(visible, teacher_score, NEG), axis=1)
    lse_s = jax.nn.logsumexp(jnp.where(visible, student_score, NEG), axis=1)
    prob_t = jnp.where(visible, jnp.exp(teacher_score - lse_t[:, None]), 0.0)
    row_kl = lax.optimization_barrier(jnp.sum(prob_t * (teacher_score - student_score), axis=1)) - lse_t + lse_s
    stats = jnp.stack([lse_t, lse_s])
    high_part = lax.optimization_barrier(stats.astype(jnp.bfloat16))
    low_part = lax.optimization_barrier((stats - high_part.astype(jnp.float32)).astype(jnp.bfloat16))
    norms = high_part.astype(jnp.float32) + low_part.astype(jnp.float32)
    weights = jnp.where(visible, jnp.exp(student_score - norms[1][:, None]) - jnp.exp(teacher_score - norms[0][:, None]), 0.0)
    weights = weights.astype(jnp.bfloat16)
    gradient = jnp.dot(weights, pupil_rows, preferred_element_type=jnp.float32) + jnp.dot(weights.T, pupil_rows, preferred_element_type=jnp.float32)
    return (jnp.sum(row_kl), gradient)

def by_heads(teach, pupil, doc_ids):
    length = teach.shape[0]
    teach_split = jnp.transpose(teach.reshape(length, RHEADS, TDIM), (1, 0, 2))
    pupil_split = jnp.transpose(pupil.reshape(length, RHEADS, HDIM), (1, 0, 2))
    totals, gradients = lax.map(lambda pair: one_head(pair[0], pair[1], doc_ids), (teach_split, pupil_split))
    merged = jnp.transpose(gradients, (1, 0, 2)).reshape(length, RHEADS * HDIM)
    return (jnp.sum(totals), merged.astype(jnp.bfloat16))

def reference(teacher_query, teacher_key, student_query, student_key, doc_ids):
    total_query, grad_query = by_heads(teacher_query, student_query, doc_ids)
    total_key, grad_key = by_heads(teacher_key, student_key, doc_ids)
    kl_loss = (total_query + total_key) / (2.0 * TOKENS * RHEADS)
    return (kl_loss, grad_query, grad_key)
```

```python
import functools
import math

import jax
import jax.numpy as jnp
from jax import lax
from jax.experimental import pallas as pl
from jax.experimental.pallas import tpu as pltpu
from jax.sharding import PartitionSpec as P

HDIM = 128
TDIM = 256
WIDE = TDIM + HDIM
NY, NZ, NX = 4, 8, 4
ROWS = 128
BLOCK = 512
TILE = 256
TOKENS = 4096
TILES = TOKENS // TILE
NEG = -1e30
LOG2E = 1.4426950408889634
LN2 = 0.6931471805599453
KT = LOG2E / math.sqrt(TDIM)
KS = LOG2E / math.sqrt(HDIM)
VMEM_LIMIT = 48 * 1024 * 1024
F32 = jnp.float32
BF16 = jnp.bfloat16
AXES = ("seq", "head")
ALL = pl.BlockSpec(memory_space=pltpu.VMEM)
SMEM = pl.BlockSpec(memory_space=pltpu.SMEM)
ANY = pl.BlockSpec(memory_space=pl.ANY)


def device(y, z, x, core):
    return (y * NZ + z) * (2 * NX) + x * 2 + core


def pairs_of(move):
    pairs = []
    for y in range(NY):
        for z in range(NZ):
            for x in range(NX):
                for core in range(2):
                    pairs.append((device(y, z, x, core), device(*move(y, z, x, core))))
    return pairs


def spread_pairs(j):
    return pairs_of(lambda y, z, x, c: (y, 4 * c + (z % 4 + j) % 4, x, z // 4))


def collect_pairs(j):
    return [(target, source) for source, target in spread_pairs(j)]


def y_pairs(step):
    return pairs_of(lambda y, z, x, c: ((y + step) % NY, z, x, c))


def x_pairs(bit):
    return pairs_of(lambda y, z, x, c: (y, z, x ^ bit, c))


CORE_PAIRS = pairs_of(lambda y, z, x, c: (y, z, x, 1 - c))


def params():
    return pltpu.CompilerParams(vmem_limit_bytes=VMEM_LIMIT)


def nt_dot(left, right):
    return lax.dot_general(left, right, (((1,), (1,)), ((), ())), preferred_element_type=F32)


def send_kernel(place, tq, tk, sq, sk, doc, o0, o1, o2, o3, held):
    below = doc[...] < lax.broadcasted_iota(jnp.int32, (128, ROWS), 0)
    counts = nt_dot(jnp.ones((16, ROWS), BF16), below.astype(F32).astype(BF16))
    for m, (teach, pupil) in enumerate(((tq, sq), (tq, sq), (tk, sk), (tk, sk))):
        h = m % 2
        held[m, 0:ROWS, 0:TDIM] = teach[:, h * TDIM:(h + 1) * TDIM]
        held[m, 0:ROWS, TDIM:WIDE] = pupil[:, h * HDIM:(h + 1) * HDIM]
        held[m, ROWS:ROWS + 16, 0:128] = counts.astype(BF16)
        held[m, ROWS:ROWS + 16, 128:WIDE] = jnp.zeros((16, 256), BF16)
    b = place[1] % 4
    for j, out in enumerate((o0, o1, o2, o3)):
        out[...] = held[(b + j) % 4]


def pack_kernel(place, r0, r1, r2, r3, out):
    m = place[1] % 4
    for j, got in enumerate((r0, r1, r2, r3)):
        b = (m - j + 4) % 4
        out[pl.ds(pl.multiple_of(b * ROWS, ROWS), ROWS), :] = got[0:ROWS, :]
    out[BLOCK:BLOCK + 16, 0:128] = r0[ROWS:ROWS + 16, 0:128] + r1[ROWS:ROWS + 16, 0:128]
    out[BLOCK:BLOCK + 16, 128:256] = r2[ROWS:ROWS + 16, 0:128] + r3[ROWS:ROWS + 16, 0:128]
    out[BLOCK:BLOCK + 16, 256:WIDE] = jnp.zeros((16, 128), BF16)


def assemble(place, parts, rows, counts, sems):
    y, core = place[0], place[2]
    copies = []
    for n, part in enumerate(parts):
        i, other = n // 2, n % 2
        from_core = core if other == 0 else 1 - core
        r = ((y - i + NY) % NY) * 2 + from_core
        copies.append(
            pltpu.make_async_copy(
                part.at[pl.ds(0, BLOCK)],
                rows.at[pl.ds(pl.multiple_of(r * BLOCK, BLOCK), BLOCK)],
                sems.at[n],
            )
        )
        copies.append(
            pltpu.make_async_copy(part.at[pl.ds(BLOCK, 16)], counts.at[n], sems.at[8 + n])
        )
    for copy in copies:
        copy.start()
    for copy in copies:
        copy.wait()
    total = jnp.zeros((16, 128), F32)
    for n in range(8):
        total = total + counts[n, :, 0:128].astype(F32) + counts[n, :, 128:256].astype(F32)
    return total[0:1]


def start_of(bounds, position):
    return jnp.max(jnp.where(bounds <= position, bounds, 0.0))


def end_of(bounds, position):
    return jnp.min(jnp.where(bounds > position, bounds, float(TOKENS)))


def tile_rows(t):
    return pl.ds(pl.multiple_of(t * TILE, TILE), TILE)


def folded(values):
    return values.reshape(TILE // 8, 8, TILE)


def norm_kernel(place, *refs):
    parts, out = refs[:8], refs[8]
    rows, counts, scores_t, scores_s, sems = refs[9:]
    bounds = assemble(place, parts, rows, counts, sems)
    r = place[0] * 2 + place[2]
    bounds_down = jnp.transpose(jnp.broadcast_to(bounds, (128, 128)))[0:16, 0:1]
    out[...] = jnp.zeros_like(out)
    for half in range(2):
        t = r if half == 0 else TILES - 1 - r
        first = t * TILE
        mine_t = rows[tile_rows(t), 0:TDIM]
        mine_s = rows[tile_rows(t), TDIM:WIDE]
        low = start_of(bounds, first.astype(F32)).astype(jnp.int32)
        high = start_of(bounds, (first + TILE - 1).astype(F32)).astype(jnp.int32)
        my_pos = first + lax.broadcasted_iota(jnp.int32, (1, TILE), 1)
        my_start = jnp.max(
            jnp.where(bounds_down <= my_pos.astype(F32), bounds_down, 0.0), axis=0, keepdims=True
        ).astype(jnp.int32)

        def score(c, tops, masked):
            t_tile = nt_dot(rows[tile_rows(c), 0:TDIM], mine_t) * KT
            s_tile = nt_dot(rows[tile_rows(c), TDIM:WIDE], mine_s) * KS
            if masked:
                pos = c * TILE + lax.broadcasted_iota(jnp.int32, (TILE, TILE), 0)
                seen = (pos <= my_pos) & (pos >= my_start)
                t_tile = jnp.where(seen, t_tile, NEG)
                s_tile = jnp.where(seen, s_tile, NEG)
            scores_t[tile_rows(c), :] = t_tile
            scores_s[tile_rows(c), :] = s_tile
            return (
                jnp.maximum(tops[0], jnp.max(folded(t_tile), axis=0)),
                jnp.maximum(tops[1], jnp.max(folded(s_tile), axis=0)),
            )

        from_tile = low // TILE
        plain_tile = jnp.minimum((high + TILE - 1) // TILE, t)
        tops = (jnp.full((8, TILE), NEG, F32), jnp.full((8, TILE), NEG, F32))
        tops = lax.fori_loop(from_tile, plain_tile, functools.partial(score, masked=True), tops)
        tops = lax.fori_loop(plain_tile, t, functools.partial(score, masked=False), tops)
        tops = score(t, tops, True)
        top_t = jnp.max(tops[0], axis=0, keepdims=True)
        top_s = jnp.max(tops[1], axis=0, keepdims=True)

        def add(c, sums):
            sum_t, sum_s, cross = sums
            t_tile = scores_t[tile_rows(c), :]
            s_tile = scores_s[tile_rows(c), :]
            p = jnp.exp2(t_tile - top_t)
            q = jnp.exp2(s_tile - top_s)
            return (
                sum_t + jnp.sum(folded(p), axis=0),
                sum_s + jnp.sum(folded(q), axis=0),
                cross + jnp.sum(folded(p * (t_tile - s_tile)), axis=0),
            )

        zero = jnp.zeros((8, TILE), F32)
        sums = lax.fori_loop(from_tile, t + 1, add, (zero, zero, zero))
        sum_t, sum_s, cross = (jnp.sum(v, axis=0, keepdims=True) for v in sums)
        lse_t = top_t * LN2 + jnp.log(sum_t)
        lse_s = top_s * LN2 + jnp.log(sum_s)
        row_kl = cross * LN2 / sum_t - lse_t + lse_s
        for k, lse in enumerate((lse_t, lse_s)):
            high_part = lse.astype(BF16).astype(F32)
            low_part = (lse - high_part).astype(BF16).astype(F32)
            out[2 * half + k:2 * half + k + 1, :] = (high_part + low_part) * LOG2E
        out[4 + half:5 + half, :] = row_kl


def grad_kernel(place, *refs):
    parts, packets, outs = refs[:8], refs[8:12], refs[12:16]
    rows, counts, norms, row_norm, acc, sems = refs[16:]
    bounds = assemble(place, parts, rows, counts, sems)
    y, core = place[0], place[2]
    r = y * 2 + core
    m = place[1] % 4
    kl = jnp.zeros((1, TILE), F32)
    for i, packet in enumerate(packets):
        for other in range(2):
            from_core = core if other == 0 else 1 - core
            from_r = ((y - i + NY) % NY) * 2 + from_core
            norms[from_r, 0:2, :] = packet[8 * other:8 * other + 2, :]
            norms[TILES - 1 - from_r, 0:2, :] = packet[8 * other + 2:8 * other + 4, :]
            kl = kl + packet[8 * other + 4:8 * other + 5, :] + packet[8 * other + 5:8 * other + 6, :]
    kl = kl[:, 0:128] + kl[:, 128:256]
    for half in range(2):
        t = 2 * r + half
        first = t * TILE
        mine_t = rows[tile_rows(t), 0:TDIM]
        mine_s = rows[tile_rows(t), TDIM:WIDE]
        for k in range(2):
            row_norm[k] = jnp.transpose(jnp.broadcast_to(norms[t, k:k + 1, :], (128, TILE)))
        my_pos = first + lax.broadcasted_iota(jnp.int32, (TILE, 1), 0)
        my_posf = my_pos.astype(F32)
        my_start = jnp.max(jnp.where(bounds <= my_posf, bounds, 0.0), axis=1, keepdims=True)
        my_end = jnp.min(jnp.where(bounds > my_posf, bounds, float(TOKENS)), axis=1, keepdims=True)
        my_start, my_end = my_start.astype(jnp.int32), my_end.astype(jnp.int32)
        start_low = start_of(bounds, first.astype(F32)).astype(jnp.int32)
        start_high = start_of(bounds, (first + TILE - 1).astype(F32)).astype(jnp.int32)
        end_low = end_of(bounds, first.astype(F32)).astype(jnp.int32)
        end_high = end_of(bounds, (first + TILE - 1).astype(F32)).astype(jnp.int32)
        acc[...] = jnp.zeros_like(acc)

        def step(c, unused, kind, masked):
            pupil = rows[tile_rows(c), TDIM:WIDE]
            t_tile = nt_dot(mine_t, rows[tile_rows(c), 0:TDIM]) * KT
            s_tile = nt_dot(mine_s, pupil) * KS
            mine = [jnp.concatenate([row_norm[k], row_norm[k]], axis=1) for k in range(2)]
            theirs = [norms[c, k:k + 1, :] for k in range(2)]
            pos = c * TILE + lax.broadcasted_iota(jnp.int32, (TILE, TILE), 1)
            if kind == "below":
                norm_t, norm_s = mine
            elif kind == "above":
                norm_t, norm_s = theirs
            else:
                own = pos <= my_pos
                norm_t, norm_s = (jnp.where(own, mine[k], theirs[k]) for k in range(2))
            weight = jnp.exp2(s_tile - norm_s) - jnp.exp2(t_tile - norm_t)
            if kind == "diagonal":
                weight = jnp.where(pos == my_pos, 2.0 * weight, weight)
            if masked:
                weight = jnp.where((pos >= my_start) & (pos < my_end), weight, 0.0)
            acc[...] += jnp.dot(weight.astype(BF16), pupil, preferred_element_type=F32)
            return unused

        def run(begin, stop, kind, masked):
            lax.fori_loop(begin, stop, functools.partial(step, kind=kind, masked=masked), 0)

        plain = jnp.minimum((start_high + TILE - 1) // TILE, t)
        run(start_low // TILE, plain, "below", True)
        run(plain, t, "below", False)
        step(t, 0, "diagonal", True)
        plain = jnp.maximum(end_low // TILE, t + 1)
        run(t + 1, plain, "above", False)
        run(plain, (end_high + TILE - 1) // TILE, "above", True)
        for q in range(2):
            b = 2 * half + q
            for j in range(4):

                @pl.when((m - j + 4) % 4 == b)
                def _():
                    outs[j][0:ROWS, :] = acc[q * ROWS:(q + 1) * ROWS, :].astype(BF16)

    high_part = kl.astype(BF16).astype(F32)
    mid_part = (kl - high_part).astype(BF16).astype(F32)
    low_part = (kl - high_part - mid_part).astype(BF16).astype(F32)
    line = lax.broadcasted_iota(jnp.int32, (16, 128), 0)
    tail = jnp.where(line == 0, high_part, jnp.where(line == 1, mid_part, jnp.where(line == 2, low_part, 0.0)))
    for j in range(4):
        outs[j][ROWS:ROWS + 16, :] = tail.astype(BF16)


def finish_kernel(place, g0, g1, g2, g3, grad_q, grad_k, kl_out, held):
    b = place[1] % 4
    kl = jnp.zeros((16, 128), F32)
    for j, got in enumerate((g0, g1, g2, g3)):
        held[(b + j) % 4] = got[0:ROWS, :]
        kl = kl + got[ROWS:ROWS + 16, :].astype(F32)
    for m in range(4):
        out = grad_q if m < 2 else grad_k
        h = m % 2
        out[:, h * HDIM:(h + 1) * HDIM] = held[m]
    kl_out[...] = kl[0:8]


def per_device(teacher_query, teacher_key, student_query, student_key, doc_ids):
    seq, head = lax.axis_index("seq"), lax.axis_index("head")
    place = jnp.stack([seq // NZ, seq % NZ, head % 2]).astype(jnp.int32)

    block = jax.ShapeDtypeStruct((ROWS + 16, WIDE), BF16)
    sends = pl.pallas_call(
        send_kernel,
        out_shape=[block] * 4,
        in_specs=[SMEM] + [ALL] * 5,
        out_specs=[ALL] * 4,
        scratch_shapes=[pltpu.VMEM((4, ROWS + 16, WIDE), BF16)],
        compiler_params=params(),
    )(place, teacher_query, teacher_key, student_query, student_key, doc_ids.reshape(1, ROWS))
    gots = [lax.ppermute(sends[j], AXES, spread_pairs(j)) for j in range(4)]
    own = pl.pallas_call(
        pack_kernel,
        out_shape=jax.ShapeDtypeStruct((BLOCK + 16, WIDE), BF16),
        in_specs=[SMEM] + [ALL] * 4,
        out_specs=ALL,
        compiler_params=params(),
    )(place, *gots)
    parts = []
    for step in range(4):
        part = own if step == 0 else lax.ppermute(own, AXES, y_pairs(step))
        parts += [part, lax.ppermute(part, AXES, CORE_PAIRS)]
    gathered = [
        pltpu.VMEM((TOKENS, WIDE), BF16),
        pltpu.VMEM((8, 16, WIDE), BF16),
    ]
    packet = pl.pallas_call(
        norm_kernel,
        out_shape=jax.ShapeDtypeStruct((8, TILE), F32),
        in_specs=[SMEM] + [ANY] * 8,
        out_specs=ALL,
        scratch_shapes=gathered
        + [
            pltpu.VMEM((TOKENS, TILE), F32),
            pltpu.VMEM((TOKENS, TILE), F32),
            pltpu.SemaphoreType.DMA((16,)),
        ],
        compiler_params=params(),
    )(place, *parts)
    both = jnp.concatenate([packet, lax.ppermute(packet, AXES, CORE_PAIRS)])
    packets = [both] + [lax.ppermute(both, AXES, y_pairs(step)) for step in (1, 2, 3)]
    grads = pl.pallas_call(
        grad_kernel,
        out_shape=[jax.ShapeDtypeStruct((ROWS + 16, HDIM), BF16)] * 4,
        in_specs=[SMEM] + [ANY] * 8 + [ALL] * 4,
        out_specs=[ALL] * 4,
        scratch_shapes=gathered
        + [
            pltpu.VMEM((TILES, 8, TILE), F32),
            pltpu.VMEM((2, TILE, 128), F32),
            pltpu.VMEM((TILE, HDIM), F32),
            pltpu.SemaphoreType.DMA((16,)),
        ],
        compiler_params=params(),
    )(place, *parts, *packets)
    backs = [lax.ppermute(grads[j], AXES, collect_pairs(j)) for j in range(4)]
    half_grad = jax.ShapeDtypeStruct((ROWS, 2 * HDIM), BF16)
    grad_query, grad_key, kl = pl.pallas_call(
        finish_kernel,
        out_shape=[half_grad, half_grad, jax.ShapeDtypeStruct((8, 128), F32)],
        in_specs=[SMEM] + [ALL] * 4,
        out_specs=[ALL] * 3,
        scratch_shapes=[pltpu.VMEM((4, ROWS, HDIM), BF16)],
        compiler_params=params(),
    )(place, *backs)
    for pairs in (x_pairs(1), x_pairs(2), CORE_PAIRS):
        kl = kl + lax.ppermute(kl, AXES, pairs)
    kl_loss = jnp.sum(kl) / (2.0 * TOKENS * 16)
    return (kl_loss, grad_query, grad_key)


def solution(mesh):
    in_specs = (P("seq", "head"), P("seq", "head"), P("seq", "head"), P("seq", "head"), P("seq"))
    out_specs = (P(), P("seq", "head"), P("seq", "head"))
    return jax.shard_map(
        per_device, mesh=mesh, in_specs=in_specs, out_specs=out_specs, check_vma=False
    )
```

```python
import functools
import math

import jax
import jax.numpy as jnp
from jax import lax
from jax.experimental import pallas as pl
from jax.experimental.pallas import tpu as pltpu
from jax.sharding import PartitionSpec as P

HDIM = 128
TDIM = 256
WIDE = TDIM + HDIM
NY, NZ, NX = 4, 8, 4
ROWS = 128
BLOCK = 512
TILE = 256
TOKENS = 4096
TILES = TOKENS // TILE
NEG = -1e30
LOG2E = 1.4426950408889634
LN2 = 0.6931471805599453
KT = LOG2E / math.sqrt(TDIM)
KS = LOG2E / math.sqrt(HDIM)
VMEM_LIMIT = 48 * 1024 * 1024
F32 = jnp.float32
BF16 = jnp.bfloat16
AXES = ("seq", "head")
ALL = pl.BlockSpec(memory_space=pltpu.VMEM)
SMEM = pl.BlockSpec(memory_space=pltpu.SMEM)
ANY = pl.BlockSpec(memory_space=pl.ANY)


def device(y, z, x, core):
    return (y * NZ + z) * (2 * NX) + x * 2 + core


def pairs_of(move):
    pairs = []
    for y in range(NY):
        for z in range(NZ):
            for x in range(NX):
                for core in range(2):
                    pairs.append((device(y, z, x, core), device(*move(y, z, x, core))))
    return pairs


def spread_pairs(j):
    return pairs_of(lambda y, z, x, c: (y, 4 * c + (z % 4 + j) % 4, x, z // 4))


def collect_pairs(j):
    return [(target, source) for source, target in spread_pairs(j)]


def y_pairs(step):
    return pairs_of(lambda y, z, x, c: ((y + step) % NY, z, x, c))


def x_pairs(bit):
    return pairs_of(lambda y, z, x, c: (y, z, x ^ bit, c))


CORE_PAIRS = pairs_of(lambda y, z, x, c: (y, z, x, 1 - c))


def params():
    return pltpu.CompilerParams(vmem_limit_bytes=VMEM_LIMIT)


def nt_dot(left, right):
    return lax.dot_general(left, right, (((1,), (1,)), ((), ())), preferred_element_type=F32)


def send_kernel(place, tq, tk, sq, sk, doc, o0, o1, o2, o3, held, docs, sems):
    copies = []
    for m, (teach, pupil) in enumerate(((tq, sq), (tq, sq), (tk, sk), (tk, sk))):
        h = m % 2
        block = held.at[m, pl.ds(0, ROWS)]
        copies.append((teach.at[:, pl.ds(h * TDIM, TDIM)], block.at[:, pl.ds(0, TDIM)]))
        copies.append((pupil.at[:, pl.ds(h * HDIM, HDIM)], block.at[:, pl.ds(TDIM, HDIM)]))
    copies.append((doc, docs))
    copies = [pltpu.make_async_copy(src, dst, sems.at[n]) for n, (src, dst) in enumerate(copies)]
    for copy in copies:
        copy.start()
    for copy in copies:
        copy.wait()
    below = docs[...] < lax.broadcasted_iota(jnp.int32, (128, ROWS), 0)
    counts = nt_dot(jnp.ones((16, ROWS), BF16), below.astype(F32).astype(BF16))
    b = place[1] % 4
    for j, out in enumerate((o0, o1, o2, o3)):
        out[0:ROWS, :] = held[(b + j) % 4]
        out[ROWS:ROWS + 16, 0:128] = counts.astype(BF16)
        out[ROWS:ROWS + 16, 128:WIDE] = jnp.zeros((16, 256), BF16)


def pack_kernel(place, r0, r1, r2, r3, out):
    m = place[1] % 4
    for j, got in enumerate((r0, r1, r2, r3)):
        b = (m - j + 4) % 4
        out[pl.ds(pl.multiple_of(b * ROWS, ROWS), ROWS), :] = got[0:ROWS, :]
    out[BLOCK:BLOCK + 16, 0:128] = r0[ROWS:ROWS + 16, 0:128] + r1[ROWS:ROWS + 16, 0:128]
    out[BLOCK:BLOCK + 16, 128:256] = r2[ROWS:ROWS + 16, 0:128] + r3[ROWS:ROWS + 16, 0:128]
    out[BLOCK:BLOCK + 16, 256:WIDE] = jnp.zeros((16, 128), BF16)


def assemble(place, parts, rows):
    y, core = place[0], place[2]
    total = jnp.zeros((16, 128), F32)
    for n, part in enumerate(parts):
        i, other = n // 2, n % 2
        from_core = core if other == 0 else 1 - core
        r = ((y - i + NY) % NY) * 2 + from_core
        rows[pl.ds(pl.multiple_of(r * BLOCK, BLOCK), BLOCK), :] = part[0:BLOCK, :]
        total = total + part[BLOCK:BLOCK + 16, 0:128].astype(F32)
        total = total + part[BLOCK:BLOCK + 16, 128:256].astype(F32)
    return total[0:1]


def start_of(bounds, position):
    return jnp.max(jnp.where(bounds <= position, bounds, 0.0))


def end_of(bounds, position):
    return jnp.min(jnp.where(bounds > position, bounds, float(TOKENS)))


def tile_rows(t):
    return pl.ds(pl.multiple_of(t * TILE, TILE), TILE)


def folded(values):
    return values.reshape(TILE // 8, 8, TILE)


def norm_kernel(place, *refs):
    parts, out = refs[:8], refs[8]
    rows, scores_t, scores_s = refs[9:]
    bounds = assemble(place, parts, rows)
    r = place[0] * 2 + place[2]
    bounds_down = jnp.transpose(jnp.broadcast_to(bounds, (128, 128)))[0:16, 0:1]
    out[...] = jnp.zeros_like(out)
    for half in range(2):
        t = r if half == 0 else TILES - 1 - r
        first = t * TILE
        mine_t = rows[tile_rows(t), 0:TDIM]
        mine_s = rows[tile_rows(t), TDIM:WIDE]
        low = start_of(bounds, first.astype(F32)).astype(jnp.int32)
        high = start_of(bounds, (first + TILE - 1).astype(F32)).astype(jnp.int32)
        my_pos = first + lax.broadcasted_iota(jnp.int32, (1, TILE), 1)
        my_start = jnp.max(
            jnp.where(bounds_down <= my_pos.astype(F32), bounds_down, 0.0), axis=0, keepdims=True
        ).astype(jnp.int32)

        def span(c, n):
            return pl.ds(pl.multiple_of(c * TILE, TILE), n * TILE)

        def eights(values):
            return values.reshape(values.shape[0] // 8, 8, TILE)

        def score(c, tops, n, masked):
            t_tile = nt_dot(rows[span(c, n), 0:TDIM], mine_t) * KT
            s_tile = nt_dot(rows[span(c, n), TDIM:WIDE], mine_s) * KS
            if masked:
                pos = c * TILE + lax.broadcasted_iota(jnp.int32, (n * TILE, TILE), 0)
                seen = (pos <= my_pos) & (pos >= my_start)
                t_tile = jnp.where(seen, t_tile, NEG)
                s_tile = jnp.where(seen, s_tile, NEG)
            scores_t[span(c, n), :] = t_tile
            scores_s[span(c, n), :] = s_tile
            return (
                jnp.maximum(tops[0], jnp.max(eights(t_tile), axis=0)),
                jnp.maximum(tops[1], jnp.max(eights(s_tile), axis=0)),
            )

        def run(begin, stop, carry, body, n=1):
            return lax.fori_loop(0, (stop - begin) // n, lambda i, v: body(begin + n * i, v, n), carry)

        def run_all(begin, stop, carry, body):
            for n in (4, 2, 1):
                middle = stop - (stop - begin) % n
                carry = run(begin, middle, carry, body, n)
                begin = middle
            return carry

        from_tile = low // TILE
        plain_tile = jnp.minimum((high + TILE - 1) // TILE, t)
        tops = (jnp.full((8, TILE), NEG, F32), jnp.full((8, TILE), NEG, F32))
        tops = run(from_tile, plain_tile, tops, functools.partial(score, masked=True))
        tops = run_all(plain_tile, t, tops, functools.partial(score, masked=False))
        tops = score(t, tops, 1, True)
        top_t = jnp.max(tops[0], axis=0, keepdims=True)
        top_s = jnp.max(tops[1], axis=0, keepdims=True)

        def add(c, sums, n):
            sum_t, sum_s, cross = sums
            t_tile = scores_t[span(c, n), :]
            s_tile = scores_s[span(c, n), :]
            p = jnp.exp2(t_tile - top_t)
            q = jnp.exp2(s_tile - top_s)
            return (
                sum_t + jnp.sum(eights(p), axis=0),
                sum_s + jnp.sum(eights(q), axis=0),
                cross + jnp.sum(eights(p * (t_tile - s_tile)), axis=0),
            )

        zero = jnp.zeros((8, TILE), F32)
        sums = run_all(from_tile, t + 1, (zero, zero, zero), add)
        sum_t, sum_s, cross = (jnp.sum(v, axis=0, keepdims=True) for v in sums)
        lse_t = top_t * LN2 + jnp.log(sum_t)
        lse_s = top_s * LN2 + jnp.log(sum_s)
        row_kl = cross * LN2 / sum_t - lse_t + lse_s
        for k, lse in enumerate((lse_t, lse_s)):
            high_part = lse.astype(BF16).astype(F32)
            low_part = (lse - high_part).astype(BF16).astype(F32)
            out[2 * half + k:2 * half + k + 1, :] = (high_part + low_part) * LOG2E
        out[4 + half:5 + half, :] = row_kl


def grad_kernel(place, *refs):
    parts, packets, outs = refs[:8], refs[8:12], refs[12:16]
    rows, norms, row_norm, acc = refs[16:]
    bounds = assemble(place, parts, rows)
    y, core = place[0], place[2]
    r = y * 2 + core
    m = place[1] % 4
    kl = jnp.zeros((1, TILE), F32)
    for i, packet in enumerate(packets):
        for other in range(2):
            from_core = core if other == 0 else 1 - core
            from_r = ((y - i + NY) % NY) * 2 + from_core
            norms[from_r, 0:2, :] = packet[8 * other:8 * other + 2, :]
            norms[TILES - 1 - from_r, 0:2, :] = packet[8 * other + 2:8 * other + 4, :]
            kl = kl + packet[8 * other + 4:8 * other + 5, :] + packet[8 * other + 5:8 * other + 6, :]
    kl = kl[:, 0:128] + kl[:, 128:256]
    first = r * BLOCK
    mine = pl.ds(pl.multiple_of(first, BLOCK), BLOCK)
    for k in range(2):
        for half in range(2):
            row_norm[k, half * TILE:(half + 1) * TILE] = jnp.transpose(
                jnp.broadcast_to(norms[2 * r + half, k:k + 1, :], (128, TILE))
            )
    my_pos = first + lax.broadcasted_iota(jnp.int32, (BLOCK, 1), 0)
    my_posf = my_pos.astype(F32)
    my_start = jnp.max(jnp.where(bounds <= my_posf, bounds, 0.0), axis=1, keepdims=True)
    my_end = jnp.min(jnp.where(bounds > my_posf, bounds, float(TOKENS)), axis=1, keepdims=True)
    my_start, my_end = my_start.astype(jnp.int32), my_end.astype(jnp.int32)
    firstf, lastf = first.astype(F32), (first + BLOCK - 1).astype(F32)
    start_low = start_of(bounds, firstf).astype(jnp.int32)
    start_high = start_of(bounds, lastf).astype(jnp.int32)
    end_low = end_of(bounds, firstf).astype(jnp.int32)
    end_high = end_of(bounds, lastf).astype(jnp.int32)
    acc[...] = jnp.zeros_like(acc)

    def columns(c, n):
        return pl.ds(pl.multiple_of(c * TILE, TILE), n * TILE)

    def step(c, n, kind, masked):
        width = n * TILE
        pupil = rows[columns(c, n), TDIM:WIDE]
        t_tile = nt_dot(rows[mine, 0:TDIM], rows[columns(c, n), 0:TDIM]) * KT
        s_tile = nt_dot(rows[mine, TDIM:WIDE], pupil) * KS
        own_norm = [jnp.concatenate([row_norm[k]] * (2 * n), axis=1) for k in range(2)]
        their_norm = [jnp.concatenate([norms[c + q, k:k + 1, :] for q in range(n)], axis=1) for k in range(2)]
        pos = c * TILE + lax.broadcasted_iota(jnp.int32, (BLOCK, width), 1)
        if kind == "below":
            norm_t, norm_s = own_norm
        elif kind == "above":
            norm_t, norm_s = their_norm
        else:
            own = pos <= my_pos
            norm_t, norm_s = (jnp.where(own, own_norm[k], their_norm[k]) for k in range(2))
        weight = jnp.exp2(s_tile - norm_s) - jnp.exp2(t_tile - norm_t)
        if kind == "diagonal":
            weight = jnp.where(pos == my_pos, 2.0 * weight, weight)
        if masked:
            weight = jnp.where((pos >= my_start) & (pos < my_end), weight, 0.0)
        acc[...] += jnp.dot(weight.astype(BF16), pupil, preferred_element_type=F32)

    def run(begin, stop, kind, masked, n=1):
        def body(i, unused):
            step(begin + n * i, n, kind, masked)
            return unused

        lax.fori_loop(0, (stop - begin) // n, body, 0)

    diag = 2 * r
    plain = jnp.minimum((start_high + TILE - 1) // TILE, diag)
    run(start_low // TILE, plain, "below", True)
    UNROLL = 2
    if UNROLL > 1:
        odd = plain + (diag - plain) % UNROLL
        run(plain, odd, "below", False)
        run(odd, diag, "below", False, UNROLL)
    else:
        run(plain, diag, "below", False)
    step(diag, 2, "diagonal", True)
    plain = jnp.maximum(end_low // TILE, diag + 2)
    if UNROLL > 1:
        odd = diag + 2 + (plain - diag - 2) % UNROLL
        run(diag + 2, odd, "above", False)
        run(odd, plain, "above", False, UNROLL)
    else:
        run(diag + 2, plain, "above", False)
    run(plain, (end_high + TILE - 1) // TILE, "above", True)
    for b in range(4):
        for j in range(4):

            @pl.when((m - j + 4) % 4 == b)
            def _():
                outs[j][0:ROWS, :] = acc[b * ROWS:(b + 1) * ROWS, :].astype(BF16)

    high_part = kl.astype(BF16).astype(F32)
    mid_part = (kl - high_part).astype(BF16).astype(F32)
    low_part = (kl - high_part - mid_part).astype(BF16).astype(F32)
    line = lax.broadcasted_iota(jnp.int32, (16, 128), 0)
    tail = jnp.where(line == 0, high_part, jnp.where(line == 1, mid_part, jnp.where(line == 2, low_part, 0.0)))
    for j in range(4):
        outs[j][ROWS:ROWS + 16, :] = tail.astype(BF16)


def finish_kernel(place, g0, g1, g2, g3, grad_q, grad_k, held):
    b = place[1] % 4
    for j, got in enumerate((g0, g1, g2, g3)):
        held[(b + j) % 4] = got[0:ROWS, :]
    for m in range(4):
        out = grad_q if m < 2 else grad_k
        h = m % 2
        out[:, h * HDIM:(h + 1) * HDIM] = held[m]


def call_norm(place, parts):
    return pl.pallas_call(
        norm_kernel,
        out_shape=jax.ShapeDtypeStruct((8, TILE), F32),
        in_specs=[SMEM] + [ALL] * 8,
        out_specs=ALL,
        scratch_shapes=[
            pltpu.VMEM((TOKENS, WIDE), BF16),
            pltpu.VMEM((TOKENS, TILE), F32),
            pltpu.VMEM((TOKENS, TILE), F32),
        ],
        compiler_params=params(),
    )(place, *parts)


def call_grad(place, parts, packets):
    return pl.pallas_call(
        grad_kernel,
        out_shape=[jax.ShapeDtypeStruct((ROWS + 16, HDIM), BF16)] * 4,
        in_specs=[SMEM] + [ALL] * 12,
        out_specs=[ALL] * 4,
        scratch_shapes=[
            pltpu.VMEM((TOKENS, WIDE), BF16),
            pltpu.VMEM((TILES, 8, TILE), F32),
            pltpu.VMEM((2, BLOCK, 128), F32),
            pltpu.VMEM((BLOCK, HDIM), F32),
        ],
        compiler_params=params(),
    )(place, *parts, *packets)


def per_device(teacher_query, teacher_key, student_query, student_key, doc_ids):
    seq, head = lax.axis_index("seq"), lax.axis_index("head")
    place = jnp.stack([seq // NZ, seq % NZ, head % 2]).astype(jnp.int32)

    block = jax.ShapeDtypeStruct((ROWS + 16, WIDE), BF16)
    sends = pl.pallas_call(
        send_kernel,
        out_shape=[block] * 4,
        in_specs=[SMEM] + [ANY] * 5,
        out_specs=[ALL] * 4,
        scratch_shapes=[
            pltpu.VMEM((4, ROWS, WIDE), BF16),
            pltpu.VMEM((1, ROWS), jnp.int32),
            pltpu.SemaphoreType.DMA((9,)),
        ],
        compiler_params=params(),
    )(place, teacher_query, teacher_key, student_query, student_key, doc_ids.reshape(1, ROWS))
    gots = [lax.ppermute(sends[j], AXES, spread_pairs(j)) for j in range(4)]
    own = pl.pallas_call(
        pack_kernel,
        out_shape=jax.ShapeDtypeStruct((BLOCK + 16, WIDE), BF16),
        in_specs=[SMEM] + [ALL] * 4,
        out_specs=ALL,
        compiler_params=params(),
    )(place, *gots)
    parts = []
    for step in range(4):
        part = own if step == 0 else lax.ppermute(own, AXES, y_pairs(step))
        parts += [part, lax.ppermute(part, AXES, CORE_PAIRS)]
    packet = call_norm(place, parts)
    both = jnp.concatenate([packet, lax.ppermute(packet, AXES, CORE_PAIRS)])
    packets = [both] + [lax.ppermute(both, AXES, y_pairs(step)) for step in (1, 2, 3)]
    grads = call_grad(place, parts, packets)
    backs = [lax.ppermute(grads[j], AXES, collect_pairs(j)) for j in range(4)]
    kl = sum(back[ROWS:ROWS + 16].astype(F32) for back in backs)
    kl = jnp.sum(kl.reshape(2, 8, HDIM), axis=0)
    kl = kl + lax.ppermute(kl, AXES, CORE_PAIRS)
    kl = kl + sum(lax.ppermute(kl, AXES, x_pairs(bits)) for bits in (1, 2, 3))
    kl_loss = jnp.sum(kl) / (2.0 * TOKENS * 16)
    half_grad = jax.ShapeDtypeStruct((ROWS, 2 * HDIM), BF16)
    grad_query, grad_key = pl.pallas_call(
        finish_kernel,
        out_shape=[half_grad, half_grad],
        in_specs=[SMEM] + [ALL] * 4,
        out_specs=[ALL] * 2,
        scratch_shapes=[pltpu.VMEM((4, ROWS, HDIM), BF16)],
        compiler_params=params(),
    )(place, *backs)
    return (kl_loss, grad_query, grad_key)


def solution(mesh):
    in_specs = (P("seq", "head"), P("seq", "head"), P("seq", "head"), P("seq", "head"), P("seq"))
    out_specs = (P(), P("seq", "head"), P("seq", "head"))
    return jax.shard_map(
        per_device, mesh=mesh, in_specs=in_specs, out_specs=out_specs, check_vma=False
    )
```

```python
import functools
import math

import jax
import jax.numpy as jnp
from jax import lax
from jax.experimental import pallas as pl
from jax.experimental.pallas import tpu as pltpu
from jax.sharding import PartitionSpec as P

HDIM = 128
TDIM = 256
WIDE = TDIM + HDIM
NY, NZ, NX = 4, 8, 4
ROWS = 128
BLOCK = 512
TILE = 256
TOKENS = 4096
TILES = TOKENS // TILE
NEG = -1e30
LOG2E = 1.4426950408889634
LN2 = 0.6931471805599453
KT = LOG2E / math.sqrt(TDIM)
KS = LOG2E / math.sqrt(HDIM)
VMEM_LIMIT = 48 * 1024 * 1024
ORDER = (0, 1, 3, 2)
PIECE = 2 * ROWS + 16
UNROLL = 2
PACK_FLOPS = 20_000_000_000
F32 = jnp.float32
BF16 = jnp.bfloat16
AXES = ("seq", "head")
ALL = pl.BlockSpec(memory_space=pltpu.VMEM)
SMEM = pl.BlockSpec(memory_space=pltpu.SMEM)
ANY = pl.BlockSpec(memory_space=pl.ANY)


def device(y, z, x, core):
    return (y * NZ + z) * (2 * NX) + x * 2 + core


def pairs_of(move):
    pairs = []
    for y in range(NY):
        for z in range(NZ):
            for x in range(NX):
                for core in range(2):
                    pairs.append((device(y, z, x, core), device(*move(y, z, x, core))))
    return pairs


def spread_pairs(j):
    return pairs_of(lambda y, z, x, c: (y, 2 * ((z // 2 + j) % 4) + c, x, z % 2))


def collect_pairs(j):
    return [(target, source) for source, target in spread_pairs(j)]


def y_pairs(step):
    return pairs_of(lambda y, z, x, c: ((y + step) % NY, z, x, c))


def x_pairs(bit):
    return pairs_of(lambda y, z, x, c: (y, z, x ^ bit, c))


CORE_PAIRS = pairs_of(lambda y, z, x, c: (y, z, x, 1 - c))


def params(limit=VMEM_LIMIT):
    return pltpu.CompilerParams(vmem_limit_bytes=limit)


def nt_dot(left, right):
    return lax.dot_general(left, right, (((1,), (1,)), ((), ())), preferred_element_type=F32)


def send_kernel(place, tq, tk, sq, sk, doc, o0, o1, o2, o3, held, docs, sems):
    copies = []
    for m, (teach, pupil) in enumerate(((tq, sq), (tq, sq), (tk, sk), (tk, sk))):
        h = m % 2
        block = held.at[m, pl.ds(0, ROWS)]
        copies.append((teach.at[:, pl.ds(h * TDIM, TDIM)], block.at[:, pl.ds(0, TDIM)]))
        copies.append((pupil.at[:, pl.ds(h * HDIM, HDIM)], block.at[:, pl.ds(TDIM, HDIM)]))
    copies.append((doc, docs))
    copies = [pltpu.make_async_copy(src, dst, sems.at[n]) for n, (src, dst) in enumerate(copies)]
    for copy in copies:
        copy.start()
    for copy in copies:
        copy.wait()
    below = docs[...] < lax.broadcasted_iota(jnp.int32, (128, ROWS), 0)
    counts = nt_dot(jnp.ones((16, ROWS), BF16), below.astype(F32).astype(BF16))
    b = place[1] // 2
    for j, out in enumerate((o0, o1, o2, o3)):
        out[0:ROWS, :] = held[(b + j) % 4]
        out[ROWS:ROWS + 16, 0:128] = counts.astype(BF16)
        out[ROWS:ROWS + 16, 128:WIDE] = jnp.zeros((16, 256), BF16)


def pack_kernel(first, second, out):
    out[0:ROWS, :] = first[0:ROWS, :]
    out[ROWS:2 * ROWS, :] = second[0:ROWS, :]
    out[2 * ROWS:PIECE, :] = first[ROWS:ROWS + 16, :] + second[ROWS:ROWS + 16, :]


def pack_both_kernel(before, first, second, out, both):
    pack_kernel(first, second, out)
    both[0:PIECE, :] = before[...]
    both[PIECE:2 * PIECE, :] = out[...]


def pieces_of(parts):
    found = []
    for other in range(2):
        for chunk in range(2):
            found.append((parts[other], chunk * PIECE, 0, other, chunk))
    for n, part in enumerate(parts[2:]):
        chunk, i, other = n // 6, n % 6 // 2 + 1, n % 2
        found.append((part, 0, i, other, chunk))
    return found


def assemble(place, parts, rows):
    y, core = place[0], place[2]
    m = place[1] // 2
    total = jnp.zeros((16, 128), F32)
    for part, base, i, other, chunk in pieces_of(parts):
        from_core = core if other == 0 else 1 - core
        from_y = (y - i + NY) % NY
        for k in range(2):
            b = (m - ORDER[2 * chunk + k] + 4) % 4
            at = (from_y * 8 + 2 * b + from_core) * ROWS
            rows[pl.ds(pl.multiple_of(at, ROWS), ROWS), :] = part[base + k * ROWS:base + (k + 1) * ROWS, :]
        total = total + part[base + 2 * ROWS:base + PIECE, 0:128].astype(F32)
    return total[0:1]


def start_of(bounds, position):
    return jnp.max(jnp.where(bounds <= position, bounds, 0.0))


def end_of(bounds, position):
    return jnp.min(jnp.where(bounds > position, bounds, float(TOKENS)))


def tile_rows(t):
    return pl.ds(pl.multiple_of(t * TILE, TILE), TILE)


def folded(values):
    return values.reshape(TILE // 8, 8, TILE)


def norm_kernel(place, *refs):
    parts, out = refs[:14], refs[14]
    rows, scores_t, scores_s = refs[15:]
    bounds = assemble(place, parts, rows)
    r = place[0] * 2 + place[2]
    bounds_down = jnp.transpose(jnp.broadcast_to(bounds, (128, 128)))[0:16, 0:1]
    out[...] = jnp.zeros_like(out)
    for half in range(2):
        t = r if half == 0 else TILES - 1 - r
        first = t * TILE
        mine_t = rows[tile_rows(t), 0:TDIM]
        mine_s = rows[tile_rows(t), TDIM:WIDE]
        low = start_of(bounds, first.astype(F32)).astype(jnp.int32)
        high = start_of(bounds, (first + TILE - 1).astype(F32)).astype(jnp.int32)
        my_pos = first + lax.broadcasted_iota(jnp.int32, (1, TILE), 1)
        my_start = jnp.max(
            jnp.where(bounds_down <= my_pos.astype(F32), bounds_down, 0.0), axis=0, keepdims=True
        ).astype(jnp.int32)

        def span(c, n):
            return pl.ds(pl.multiple_of(c * TILE, TILE), n * TILE)

        def eights(values):
            return values.reshape(values.shape[0] // 8, 8, TILE)

        def score(c, tops, n, masked):
            t_tile = nt_dot(rows[span(c, n), 0:TDIM], mine_t) * KT
            s_tile = nt_dot(rows[span(c, n), TDIM:WIDE], mine_s) * KS
            if masked:
                pos = c * TILE + lax.broadcasted_iota(jnp.int32, (n * TILE, TILE), 0)
                seen = (pos <= my_pos) & (pos >= my_start)
                t_tile = jnp.where(seen, t_tile, NEG)
                s_tile = jnp.where(seen, s_tile, NEG)
            scores_t[span(c, n), :] = t_tile
            scores_s[span(c, n), :] = s_tile
            return (
                jnp.maximum(tops[0], jnp.max(eights(t_tile), axis=0)),
                jnp.maximum(tops[1], jnp.max(eights(s_tile), axis=0)),
            )

        def run(begin, stop, carry, body, n=1):
            return lax.fori_loop(0, (stop - begin) // n, lambda i, v: body(begin + n * i, v, n), carry)

        def run_all(begin, stop, carry, body):
            for n in (4, 2, 1):
                middle = stop - (stop - begin) % n
                carry = run(begin, middle, carry, body, n)
                begin = middle
            return carry

        from_tile = low // TILE
        plain_tile = jnp.minimum((high + TILE - 1) // TILE, t)
        tops = (jnp.full((8, TILE), NEG, F32), jnp.full((8, TILE), NEG, F32))
        tops = run_all(from_tile, plain_tile, tops, functools.partial(score, masked=True))
        tops = run_all(plain_tile, t, tops, functools.partial(score, masked=False))
        tops = score(t, tops, 1, True)
        top_t = jnp.max(tops[0], axis=0, keepdims=True)
        top_s = jnp.max(tops[1], axis=0, keepdims=True)

        def add(c, sums, n):
            sum_t, sum_s, cross = sums
            t_tile = scores_t[span(c, n), :]
            s_tile = scores_s[span(c, n), :]
            p = jnp.exp2(t_tile - top_t)
            q = jnp.exp2(s_tile - top_s)
            return (
                sum_t + jnp.sum(eights(p), axis=0),
                sum_s + jnp.sum(eights(q), axis=0),
                cross + jnp.sum(eights(p * (t_tile - s_tile)), axis=0),
            )

        zero = jnp.zeros((8, TILE), F32)
        sums = run_all(from_tile, t + 1, (zero, zero, zero), add)
        sum_t, sum_s, cross = (jnp.sum(v, axis=0, keepdims=True) for v in sums)
        lse_t = top_t * LN2 + jnp.log(sum_t)
        lse_s = top_s * LN2 + jnp.log(sum_s)
        row_kl = cross * LN2 / sum_t - lse_t + lse_s
        for k, lse in enumerate((lse_t, lse_s)):
            high_part = lse.astype(BF16).astype(F32)
            low_part = (lse - high_part).astype(BF16).astype(F32)
            out[2 * half + k:2 * half + k + 1, :] = (high_part + low_part) * LOG2E
        out[4 + half:5 + half, :] = row_kl


def grad_kernel(place, *refs):
    parts, packets, outs = refs[:14], refs[14:18], refs[18:22]
    rows, norms, row_norm, acc, mine = refs[22:]
    bounds = assemble(place, parts, rows)
    y, core = place[0], place[2]
    m = place[1] // 2
    kl = jnp.zeros((1, TILE), F32)
    for i, packet in enumerate(packets):
        for other in range(2):
            from_core = core if other == 0 else 1 - core
            from_r = ((y - i + NY) % NY) * 2 + from_core
            norms[from_r, 0:2, :] = packet[8 * other:8 * other + 2, :]
            norms[TILES - 1 - from_r, 0:2, :] = packet[8 * other + 2:8 * other + 4, :]
            kl = kl + packet[8 * other + 4:8 * other + 5, :] + packet[8 * other + 5:8 * other + 6, :]
    kl = kl[:, 0:128] + kl[:, 128:256]
    first = y * (2 * BLOCK) + core * ROWS
    last = first + 7 * ROWS - 1
    for b in range(4):
        sub = slice(b * ROWS, (b + 1) * ROWS)
        mine[sub, :] = rows[pl.ds(pl.multiple_of(first + 2 * b * ROWS, ROWS), ROWS), :]
        for k in range(2):
            line = norms[4 * y + b, k:k + 1, :]
            line = jnp.where(core == 0, line[:, 0:ROWS], line[:, ROWS:TILE])
            row_norm[k, sub] = jnp.transpose(jnp.broadcast_to(line, (ROWS, ROWS)))
    my_index = lax.broadcasted_iota(jnp.int32, (BLOCK, 1), 0)
    my_pos = first + my_index + (my_index // ROWS) * ROWS
    my_posf = my_pos.astype(F32)
    my_start = jnp.max(jnp.where(bounds <= my_posf, bounds, 0.0), axis=1, keepdims=True)
    my_end = jnp.min(jnp.where(bounds > my_posf, bounds, float(TOKENS)), axis=1, keepdims=True)
    my_start, my_end = my_start.astype(jnp.int32), my_end.astype(jnp.int32)
    firstf, lastf = first.astype(F32), last.astype(F32)
    start_low = start_of(bounds, firstf).astype(jnp.int32)
    start_high = start_of(bounds, lastf).astype(jnp.int32)
    end_low = end_of(bounds, firstf).astype(jnp.int32)
    end_high = end_of(bounds, lastf).astype(jnp.int32)
    acc[...] = jnp.zeros_like(acc)

    def columns(c, n):
        return pl.ds(pl.multiple_of(c * TILE, TILE), n * TILE)

    def step(c, n, kind, masked):
        width = n * TILE
        pupil = rows[columns(c, n), TDIM:WIDE]
        t_tile = nt_dot(mine[:, 0:TDIM], rows[columns(c, n), 0:TDIM]) * KT
        s_tile = nt_dot(mine[:, TDIM:WIDE], pupil) * KS
        own_norm = [jnp.concatenate([row_norm[k]] * (2 * n), axis=1) for k in range(2)]
        their_norm = [jnp.concatenate([norms[c + q, k:k + 1, :] for q in range(n)], axis=1) for k in range(2)]
        pos = c * TILE + lax.broadcasted_iota(jnp.int32, (BLOCK, width), 1)
        if kind == "below":
            norm_t, norm_s = own_norm
        elif kind == "above":
            norm_t, norm_s = their_norm
        else:
            own = pos <= my_pos
            norm_t, norm_s = (jnp.where(own, own_norm[k], their_norm[k]) for k in range(2))
        weight = jnp.exp2(s_tile - norm_s) - jnp.exp2(t_tile - norm_t)
        if kind == "diagonal":
            weight = jnp.where(pos == my_pos, 2.0 * weight, weight)
        if masked:
            weight = jnp.where((pos >= my_start) & (pos < my_end), weight, 0.0)
        acc[...] += jnp.dot(weight.astype(BF16), pupil, preferred_element_type=F32)

    def run(begin, stop, kind, masked, n=1):
        def body(i, unused):
            step(begin + n * i, n, kind, masked)
            return unused

        lax.fori_loop(0, (stop - begin) // n, body, 0)

    diag = 4 * y
    plain = jnp.minimum((start_high + TILE - 1) // TILE, diag)
    begin = start_low // TILE
    odd = plain - (plain - begin) % UNROLL
    run(begin, odd, "below", True, UNROLL)
    run(odd, plain, "below", True)
    odd = plain + (diag - plain) % UNROLL
    run(plain, odd, "below", False)
    run(odd, diag, "below", False, UNROLL)
    run(diag, diag + 4, "diagonal", True, 2)
    plain = jnp.maximum(end_low // TILE, diag + 4)
    odd = diag + 4 + (plain - diag - 4) % UNROLL
    run(diag + 4, odd, "above", False)
    run(odd, plain, "above", False, UNROLL)
    stop = (end_high + TILE - 1) // TILE
    odd = plain + (stop - plain) % UNROLL
    run(plain, odd, "above", True)
    run(odd, stop, "above", True, UNROLL)
    for b in range(4):
        for j in range(4):

            @pl.when((m - j + 4) % 4 == b)
            def _():
                outs[j][0:ROWS, :] = acc[b * ROWS:(b + 1) * ROWS, :].astype(BF16)

    high_part = kl.astype(BF16).astype(F32)
    mid_part = (kl - high_part).astype(BF16).astype(F32)
    low_part = (kl - high_part - mid_part).astype(BF16).astype(F32)
    line = lax.broadcasted_iota(jnp.int32, (16, 128), 0)
    tail = jnp.where(line == 0, high_part, jnp.where(line == 1, mid_part, jnp.where(line == 2, low_part, 0.0)))
    for j in range(4):
        outs[j][ROWS:ROWS + 16, :] = tail.astype(BF16)


def finish_kernel(place, g0, g1, g2, g3, grad_q, grad_k, held):
    b = place[1] // 2
    for j, got in enumerate((g0, g1, g2, g3)):
        held[(b + j) % 4] = got[0:ROWS, :]
    for m in range(4):
        out = grad_q if m < 2 else grad_k
        h = m % 2
        out[:, h * HDIM:(h + 1) * HDIM] = held[m]


def call_norm(place, parts):
    return pl.pallas_call(
        norm_kernel,
        out_shape=jax.ShapeDtypeStruct((8, TILE), F32),
        in_specs=[SMEM] + [ALL] * 14,
        out_specs=ALL,
        scratch_shapes=[
            pltpu.VMEM((TOKENS, WIDE), BF16),
            pltpu.VMEM((TOKENS, TILE), F32),
            pltpu.VMEM((TOKENS, TILE), F32),
        ],
        compiler_params=params(),
    )(place, *parts)


def call_grad(place, parts, packets):
    return pl.pallas_call(
        grad_kernel,
        out_shape=[jax.ShapeDtypeStruct((ROWS + 16, HDIM), BF16)] * 4,
        in_specs=[SMEM] + [ALL] * 18,
        out_specs=[ALL] * 4,
        scratch_shapes=[
            pltpu.VMEM((TOKENS, WIDE), BF16),
            pltpu.VMEM((TILES, 8, TILE), F32),
            pltpu.VMEM((2, BLOCK, 128), F32),
            pltpu.VMEM((BLOCK, HDIM), F32),
            pltpu.VMEM((BLOCK, WIDE), BF16),
        ],
        compiler_params=params(),
    )(place, *parts, *packets)


def per_device(teacher_query, teacher_key, student_query, student_key, doc_ids):
    seq, head = lax.axis_index("seq"), lax.axis_index("head")
    place = jnp.stack([seq // NZ, seq % NZ, head % 2]).astype(jnp.int32)

    block = jax.ShapeDtypeStruct((ROWS + 16, WIDE), BF16)
    sends = pl.pallas_call(
        send_kernel,
        out_shape=[block] * 4,
        in_specs=[SMEM] + [ANY] * 5,
        out_specs=[ALL] * 4,
        scratch_shapes=[
            pltpu.VMEM((4, ROWS, WIDE), BF16),
            pltpu.VMEM((1, ROWS), jnp.int32),
            pltpu.SemaphoreType.DMA((9,)),
        ],
        compiler_params=params(60 * 1024 * 1024),
    )(place, teacher_query, teacher_key, student_query, student_key, doc_ids.reshape(1, ROWS))
    gots = [lax.ppermute(sends[j], AXES, spread_pairs(j)) for j in ORDER]
    piece = jax.ShapeDtypeStruct((PIECE, WIDE), BF16)
    own_a = pl.pallas_call(
        pack_kernel,
        out_shape=piece,
        in_specs=[ALL] * 2,
        out_specs=ALL,
        compiler_params=params(),
        cost_estimate=pl.CostEstimate(
            flops=PACK_FLOPS, bytes_accessed=4 * PIECE * WIDE, transcendentals=0
        ),
    )(*gots[0:2])
    own_b, own = pl.pallas_call(
        pack_both_kernel,
        out_shape=[piece, jax.ShapeDtypeStruct((2 * PIECE, WIDE), BF16)],
        in_specs=[ALL] * 3,
        out_specs=[ALL] * 2,
        compiler_params=params(),
    )(own_a, *gots[2:4])
    parts = [own, lax.ppermute(own, AXES, CORE_PAIRS)]
    for mine in (own_a, own_b):
        for step in (1, 2, 3):
            part = lax.ppermute(mine, AXES, y_pairs(step))
            parts += [part, lax.ppermute(part, AXES, CORE_PAIRS)]
    packet = call_norm(place, parts)
    both = jnp.concatenate([packet, lax.ppermute(packet, AXES, CORE_PAIRS)])
    packets = [both] + [lax.ppermute(both, AXES, y_pairs(step)) for step in (1, 2, 3)]
    grads = call_grad(place, parts, packets)
    backs = [lax.ppermute(grads[j], AXES, collect_pairs(j)) for j in range(4)]
    kl = sum(back[ROWS:ROWS + 16].astype(F32) for back in backs)
    kl = jnp.sum(kl.reshape(2, 8, HDIM), axis=0)
    kl = kl + lax.ppermute(kl, AXES, CORE_PAIRS)
    kl = kl + sum(lax.ppermute(kl, AXES, x_pairs(bits)) for bits in (1, 2, 3))
    kl_loss = jnp.sum(kl) / (2.0 * TOKENS * 16)
    half_grad = jax.ShapeDtypeStruct((ROWS, 2 * HDIM), BF16)
    grad_query, grad_key = pl.pallas_call(
        finish_kernel,
        out_shape=[half_grad, half_grad],
        in_specs=[SMEM] + [ALL] * 4,
        out_specs=[ALL] * 2,
        scratch_shapes=[pltpu.VMEM((4, ROWS, HDIM), BF16)],
        compiler_params=params(),
    )(place, *backs)
    return (kl_loss, grad_query, grad_key)


def solution(mesh):
    in_specs = (P("seq", "head"), P("seq", "head"), P("seq", "head"), P("seq", "head"), P("seq"))
    out_specs = (P(), P("seq", "head"), P("seq", "head"))
    return jax.shard_map(
        per_device, mesh=mesh, in_specs=in_specs, out_specs=out_specs, check_vma=False
    )
```

```python
import functools
import math

import jax
import jax.numpy as jnp
from jax import lax
from jax.experimental import pallas as pl
from jax.experimental.pallas import tpu as pltpu
from jax.sharding import PartitionSpec as P

HDIM = 128
TDIM = 256
WIDE = TDIM + HDIM
NY, NZ, NX = 4, 8, 4
ROWS = 128
BLOCK = 512
TILE = 256
TOKENS = 4096
TILES = TOKENS // TILE
NEG = -1e30
LOG2E = 1.4426950408889634
LN2 = 0.6931471805599453
KT = LOG2E / math.sqrt(TDIM)
KS = LOG2E / math.sqrt(HDIM)
VMEM_LIMIT = 48 * 1024 * 1024
ORDER = (0, 1, 3, 2)
PIECE = 2 * ROWS + 16
UNROLL = 2
PACK_FLOPS = 20_000_000_000
F32 = jnp.float32
BF16 = jnp.bfloat16
AXES = ("seq", "head")
ALL = pl.BlockSpec(memory_space=pltpu.VMEM)
ANY = pl.BlockSpec(memory_space=pl.ANY)


def device(y, z, x, core):
    return (y * NZ + z) * (2 * NX) + x * 2 + core


def pairs_of(move):
    pairs = []
    for y in range(NY):
        for z in range(NZ):
            for x in range(NX):
                for core in range(2):
                    pairs.append((device(y, z, x, core), device(*move(y, z, x, core))))
    return pairs


def spread_pairs(j):
    return pairs_of(lambda y, z, x, c: (y, 2 * ((z // 2 + j) % 4) + c, x, z % 2))


def collect_pairs(j):
    return [(target, source) for source, target in spread_pairs(j)]


def near_pairs(sign):
    return pairs_of(lambda y, z, x, c: ((y + sign * (1 - 2 * c)) % NY, z, x, c))


def y_pairs(step):
    return pairs_of(lambda y, z, x, c: ((y + step) % NY, z, x, c))


def x_pairs(bit):
    return pairs_of(lambda y, z, x, c: (y, z, x ^ bit, c))


CORE_PAIRS = pairs_of(lambda y, z, x, c: (y, z, x, 1 - c))


def placed():
    seq, head = lax.axis_index("seq"), lax.axis_index("head")
    return (lax.div(seq, NZ), lax.rem(seq, NZ), lax.rem(head, 2))


def params(limit=VMEM_LIMIT):
    return pltpu.CompilerParams(vmem_limit_bytes=limit)


def nt_dot(left, right):
    return lax.dot_general(left, right, (((1,), (1,)), ((), ())), preferred_element_type=F32)


def send_kernel(tq, tk, sq, sk, doc, o0, o1, o2, o3, held, docs, sems):
    copies = []
    for m, (teach, pupil) in enumerate(((tq, sq), (tq, sq), (tk, sk), (tk, sk))):
        h = m % 2
        block = held.at[m, pl.ds(0, ROWS)]
        copies.append((teach.at[:, pl.ds(h * TDIM, TDIM)], block.at[:, pl.ds(0, TDIM)]))
        copies.append((pupil.at[:, pl.ds(h * HDIM, HDIM)], block.at[:, pl.ds(TDIM, HDIM)]))
    copies.append((doc, docs))
    copies = [pltpu.make_async_copy(src, dst, sems.at[n]) for n, (src, dst) in enumerate(copies)]
    for copy in reversed(copies):
        copy.start()
    copies.pop().wait()
    below = docs[...] < lax.broadcasted_iota(jnp.int32, (128, ROWS), 0)
    counts = nt_dot(jnp.ones((16, ROWS), BF16), below.astype(F32).astype(BF16))
    for out in (o0, o1, o2, o3):
        out[ROWS:ROWS + 16, 0:128] = counts.astype(BF16)
        out[ROWS:ROWS + 16, 128:WIDE] = jnp.zeros((16, 256), BF16)
    for copy in copies:
        copy.wait()
    b = placed()[1] // 2
    for j, out in enumerate((o0, o1, o2, o3)):
        out[0:ROWS, :] = held[(b + j) % 4]


def pack_kernel(first, second, out):
    out[0:ROWS, :] = first[0:ROWS, :]
    out[ROWS:2 * ROWS, :] = second[0:ROWS, :]
    out[2 * ROWS:PIECE, :] = first[ROWS:ROWS + 16, :] + second[ROWS:ROWS + 16, :]


def pack_both_kernel(before, first, second, out, both):
    pack_kernel(first, second, out)
    both[0:PIECE, :] = before[...]
    both[PIECE:2 * PIECE, :] = out[...]


def pieces_of(parts):
    found = []
    for other in range(2):
        for chunk in range(2):
            found.append((parts[other], chunk * PIECE, 0, other, chunk))
    for n, part in enumerate(parts[2:]):
        chunk, step, other = n // 6, (1, -1, 2)[n % 6 // 2], n % 2
        found.append((part, 0, step, other, chunk))
    return found


def assemble(parts, rows):
    y, z, core = placed()
    m = z // 2
    total = jnp.zeros((16, 128), F32)
    for part, base, step, other, chunk in pieces_of(parts):
        from_core = core if other == 0 else 1 - core
        from_y = (y - step * (1 - 2 * from_core) + NY) % NY
        for k in range(2):
            b = (m - ORDER[2 * chunk + k] + 4) % 4
            at = (from_y * 8 + 2 * b + from_core) * ROWS
            rows[pl.ds(pl.multiple_of(at, ROWS), ROWS), :] = part[base + k * ROWS:base + (k + 1) * ROWS, :]
        total = total + part[base + 2 * ROWS:base + PIECE, 0:128].astype(F32)
    return total[0:1]


def start_of(bounds, position):
    return jnp.max(jnp.where(bounds <= position, bounds, 0.0))


def end_of(bounds, position):
    return jnp.min(jnp.where(bounds > position, bounds, float(TOKENS)))


def tile_rows(t):
    return pl.ds(pl.multiple_of(t * TILE, TILE), TILE)


def folded(values):
    return values.reshape(TILE // 8, 8, TILE)


def norm_kernel(*refs):
    parts, out = refs[:14], refs[14]
    rows, scores_t, scores_s = refs[15:]
    bounds = assemble(parts, rows)
    y, z, core = placed()
    r = y * 2 + core
    bounds_down = jnp.transpose(jnp.broadcast_to(bounds, (128, 128)))[0:16, 0:1]
    out[...] = jnp.zeros_like(out)
    for half in range(2):
        t = r if half == 0 else TILES - 1 - r
        first = t * TILE
        mine_t = rows[tile_rows(t), 0:TDIM]
        mine_s = rows[tile_rows(t), TDIM:WIDE]
        low = start_of(bounds, first.astype(F32)).astype(jnp.int32)
        high = start_of(bounds, (first + TILE - 1).astype(F32)).astype(jnp.int32)
        my_pos = first + lax.broadcasted_iota(jnp.int32, (1, TILE), 1)
        my_start = jnp.max(
            jnp.where(bounds_down <= my_pos.astype(F32), bounds_down, 0.0), axis=0, keepdims=True
        ).astype(jnp.int32)

        def span(c, n):
            return pl.ds(pl.multiple_of(c * TILE, TILE), n * TILE)

        def eights(values):
            return values.reshape(values.shape[0] // 8, 8, TILE)

        def score(c, tops, n, masked):
            t_tile = nt_dot(rows[span(c, n), 0:TDIM], mine_t) * KT
            s_tile = nt_dot(rows[span(c, n), TDIM:WIDE], mine_s) * KS
            if masked:
                pos = c * TILE + lax.broadcasted_iota(jnp.int32, (n * TILE, TILE), 0)
                seen = (pos <= my_pos) & (pos >= my_start)
                t_tile = jnp.where(seen, t_tile, NEG)
                s_tile = jnp.where(seen, s_tile, NEG)
            scores_t[span(c, n), :] = t_tile
            scores_s[span(c, n), :] = s_tile
            return (
                jnp.maximum(tops[0], jnp.max(eights(t_tile), axis=0)),
                jnp.maximum(tops[1], jnp.max(eights(s_tile), axis=0)),
            )

        def run(begin, stop, carry, body, n=1):
            return lax.fori_loop(0, (stop - begin) // n, lambda i, v: body(begin + n * i, v, n), carry)

        def run_all(begin, stop, carry, body):
            for n in (4, 2, 1):
                middle = stop - (stop - begin) % n
                carry = run(begin, middle, carry, body, n)
                begin = middle
            return carry

        from_tile = low // TILE
        plain_tile = jnp.minimum((high + TILE - 1) // TILE, t)
        tops = (jnp.full((8, TILE), NEG, F32), jnp.full((8, TILE), NEG, F32))
        tops = run_all(from_tile, plain_tile, tops, functools.partial(score, masked=True))
        tops = run_all(plain_tile, t, tops, functools.partial(score, masked=False))
        tops = score(t, tops, 1, True)
        top_t = jnp.max(tops[0], axis=0, keepdims=True)
        top_s = jnp.max(tops[1], axis=0, keepdims=True)

        def add(c, sums, n):
            sum_t, sum_s, cross = sums
            t_tile = scores_t[span(c, n), :]
            s_tile = scores_s[span(c, n), :]
            p = jnp.exp2(t_tile - top_t)
            q = jnp.exp2(s_tile - top_s)
            return (
                sum_t + jnp.sum(eights(p), axis=0),
                sum_s + jnp.sum(eights(q), axis=0),
                cross + jnp.sum(eights(p * (t_tile - s_tile)), axis=0),
            )

        zero = jnp.zeros((8, TILE), F32)
        sums = run_all(from_tile, t + 1, (zero, zero, zero), add)
        sum_t, sum_s, cross = (jnp.sum(v, axis=0, keepdims=True) for v in sums)
        lse_t = top_t * LN2 + jnp.log(sum_t)
        lse_s = top_s * LN2 + jnp.log(sum_s)
        row_kl = cross * LN2 / sum_t - lse_t + lse_s
        for k, lse in enumerate((lse_t, lse_s)):
            high_part = lse.astype(BF16).astype(F32)
            low_part = (lse - high_part).astype(BF16).astype(F32)
            out[2 * half + k:2 * half + k + 1, :] = (high_part + low_part) * LOG2E
        out[4 + half:5 + half, :] = row_kl


def grad_kernel(*refs):
    parts, packets, outs = refs[:14], refs[14:18], refs[18:22]
    rows, norms, row_norm, acc, mine = refs[22:]
    bounds = assemble(parts, rows)
    y, z, core = placed()
    m = z // 2
    kl = jnp.zeros((1, TILE), F32)
    for i, packet in enumerate(packets):
        for other in range(2):
            from_core = core if other == 0 else 1 - core
            from_r = ((y - i + NY) % NY) * 2 + from_core
            norms[from_r, 0:2, :] = packet[8 * other:8 * other + 2, :]
            norms[TILES - 1 - from_r, 0:2, :] = packet[8 * other + 2:8 * other + 4, :]
            kl = kl + packet[8 * other + 4:8 * other + 5, :] + packet[8 * other + 5:8 * other + 6, :]
    kl = kl[:, 0:128] + kl[:, 128:256]
    first = y * (2 * BLOCK) + core * ROWS
    last = first + 7 * ROWS - 1
    for b in range(4):
        sub = slice(b * ROWS, (b + 1) * ROWS)
        mine[sub, :] = rows[pl.ds(pl.multiple_of(first + 2 * b * ROWS, ROWS), ROWS), :]
        for k in range(2):
            line = norms[4 * y + b, k:k + 1, :]
            line = jnp.where(core == 0, line[:, 0:ROWS], line[:, ROWS:TILE])
            row_norm[k, sub] = jnp.transpose(jnp.broadcast_to(line, (ROWS, ROWS)))
    my_index = lax.broadcasted_iota(jnp.int32, (BLOCK, 1), 0)
    my_pos = first + my_index + (my_index // ROWS) * ROWS
    my_posf = my_pos.astype(F32)
    my_start = jnp.max(jnp.where(bounds <= my_posf, bounds, 0.0), axis=1, keepdims=True)
    my_end = jnp.min(jnp.where(bounds > my_posf, bounds, float(TOKENS)), axis=1, keepdims=True)
    my_start, my_end = my_start.astype(jnp.int32), my_end.astype(jnp.int32)
    firstf, lastf = first.astype(F32), last.astype(F32)
    start_low = start_of(bounds, firstf).astype(jnp.int32)
    start_high = start_of(bounds, lastf).astype(jnp.int32)
    end_low = end_of(bounds, firstf).astype(jnp.int32)
    end_high = end_of(bounds, lastf).astype(jnp.int32)
    acc[...] = jnp.zeros_like(acc)

    def columns(c, n):
        return pl.ds(pl.multiple_of(c * TILE, TILE), n * TILE)

    def step(c, n, kind, masked):
        width = n * TILE
        pupil = rows[columns(c, n), TDIM:WIDE]
        t_tile = nt_dot(mine[:, 0:TDIM], rows[columns(c, n), 0:TDIM]) * KT
        s_tile = nt_dot(mine[:, TDIM:WIDE], pupil) * KS
        own_norm = [jnp.concatenate([row_norm[k]] * (2 * n), axis=1) for k in range(2)]
        their_norm = [jnp.concatenate([norms[c + q, k:k + 1, :] for q in range(n)], axis=1) for k in range(2)]
        pos = c * TILE + lax.broadcasted_iota(jnp.int32, (BLOCK, width), 1)
        if kind == "below":
            norm_t, norm_s = own_norm
        elif kind == "above":
            norm_t, norm_s = their_norm
        else:
            own = pos <= my_pos
            norm_t, norm_s = (jnp.where(own, own_norm[k], their_norm[k]) for k in range(2))
        weight = jnp.exp2(s_tile - norm_s) - jnp.exp2(t_tile - norm_t)
        if kind == "diagonal":
            weight = jnp.where(pos == my_pos, 2.0 * weight, weight)
        if masked:
            weight = jnp.where((pos >= my_start) & (pos < my_end), weight, 0.0)
        acc[...] += jnp.dot(weight.astype(BF16), pupil, preferred_element_type=F32)

    def run(begin, stop, kind, masked, n=1):
        def body(i, unused):
            step(begin + n * i, n, kind, masked)
            return unused

        lax.fori_loop(0, (stop - begin) // n, body, 0)

    diag = 4 * y
    plain = jnp.minimum((start_high + TILE - 1) // TILE, diag)
    begin = start_low // TILE
    odd = plain - (plain - begin) % UNROLL
    run(begin, odd, "below", True, UNROLL)
    run(odd, plain, "below", True)
    odd = plain + (diag - plain) % UNROLL
    run(plain, odd, "below", False)
    run(odd, diag, "below", False, UNROLL)
    run(diag, diag + 4, "diagonal", True, 2)
    plain = jnp.maximum(end_low // TILE, diag + 4)
    odd = diag + 4 + (plain - diag - 4) % UNROLL
    run(diag + 4, odd, "above", False)
    run(odd, plain, "above", False, UNROLL)
    stop = (end_high + TILE - 1) // TILE
    odd = plain + (stop - plain) % UNROLL
    run(plain, odd, "above", True)
    run(odd, stop, "above", True, UNROLL)
    for b in range(4):
        for j in range(4):

            @pl.when((m - j + 4) % 4 == b)
            def _():
                outs[j][0:ROWS, :] = acc[b * ROWS:(b + 1) * ROWS, :].astype(BF16)

    high_part = kl.astype(BF16).astype(F32)
    mid_part = (kl - high_part).astype(BF16).astype(F32)
    low_part = (kl - high_part - mid_part).astype(BF16).astype(F32)
    line = lax.broadcasted_iota(jnp.int32, (16, 128), 0)
    tail = jnp.where(line == 0, high_part, jnp.where(line == 1, mid_part, jnp.where(line == 2, low_part, 0.0)))
    for j in range(4):
        outs[j][ROWS:ROWS + 16, :] = tail.astype(BF16)


def finish_kernel(g0, g1, g2, g3, grad_q, grad_k, held):
    b = placed()[1] // 2
    for j, got in enumerate((g0, g1, g2, g3)):
        held[(b + j) % 4] = got[0:ROWS, :]
    for m in range(4):
        out = grad_q if m < 2 else grad_k
        h = m % 2
        out[:, h * HDIM:(h + 1) * HDIM] = held[m]


def call_norm(parts):
    return pl.pallas_call(
        norm_kernel,
        out_shape=jax.ShapeDtypeStruct((8, TILE), F32),
        in_specs=[ALL] * 14,
        out_specs=ALL,
        scratch_shapes=[
            pltpu.VMEM((TOKENS, WIDE), BF16),
            pltpu.VMEM((TOKENS, TILE), F32),
            pltpu.VMEM((TOKENS, TILE), F32),
        ],
        compiler_params=params(),
    )(*parts)


def call_grad(parts, packets):
    return pl.pallas_call(
        grad_kernel,
        out_shape=[jax.ShapeDtypeStruct((ROWS + 16, HDIM), BF16)] * 4,
        in_specs=[ALL] * 18,
        out_specs=[ALL] * 4,
        scratch_shapes=[
            pltpu.VMEM((TOKENS, WIDE), BF16),
            pltpu.VMEM((TILES, 8, TILE), F32),
            pltpu.VMEM((2, BLOCK, 128), F32),
            pltpu.VMEM((BLOCK, HDIM), F32),
            pltpu.VMEM((BLOCK, WIDE), BF16),
        ],
        compiler_params=params(),
    )(*parts, *packets)


def per_device(teacher_query, teacher_key, student_query, student_key, doc_ids):
    block = jax.ShapeDtypeStruct((ROWS + 16, WIDE), BF16)
    sends = pl.pallas_call(
        send_kernel,
        out_shape=[block] * 4,
        in_specs=[ANY] * 5,
        out_specs=[ALL] * 4,
        scratch_shapes=[
            pltpu.VMEM((4, ROWS, WIDE), BF16),
            pltpu.VMEM((1, ROWS), jnp.int32),
            pltpu.SemaphoreType.DMA((9,)),
        ],
        compiler_params=params(60 * 1024 * 1024),
    )(teacher_query, teacher_key, student_query, student_key, doc_ids.reshape(1, ROWS))
    gots = [lax.ppermute(sends[j], AXES, spread_pairs(j)) for j in ORDER]
    piece = jax.ShapeDtypeStruct((PIECE, WIDE), BF16)
    own_a = pl.pallas_call(
        pack_kernel,
        out_shape=piece,
        in_specs=[ALL] * 2,
        out_specs=ALL,
        compiler_params=params(),
        cost_estimate=pl.CostEstimate(
            flops=PACK_FLOPS, bytes_accessed=4 * PIECE * WIDE, transcendentals=0
        ),
    )(*gots[0:2])
    own_b, own = pl.pallas_call(
        pack_both_kernel,
        out_shape=[piece, jax.ShapeDtypeStruct((2 * PIECE, WIDE), BF16)],
        in_specs=[ALL] * 3,
        out_specs=[ALL] * 2,
        compiler_params=params(),
    )(own_a, *gots[2:4])
    parts = [own, lax.ppermute(own, AXES, CORE_PAIRS)]
    nears = [lax.ppermute(mine, AXES, near_pairs(1)) for mine in (own_a, own_b)]
    fars = [lax.ppermute(mine, AXES, near_pairs(-1)) for mine in (own_a, own_b)]
    opposites = [lax.ppermute(near, AXES, near_pairs(1)) for near in nears]
    for trio in zip(nears, fars, opposites):
        for part in trio:
            parts += [part, lax.ppermute(part, AXES, CORE_PAIRS)]
    packet = call_norm(parts)
    both = jnp.concatenate([packet, lax.ppermute(packet, AXES, CORE_PAIRS)])
    packets = [both] + [lax.ppermute(both, AXES, y_pairs(step)) for step in (1, 2, 3)]
    grads = call_grad(parts, packets)
    backs = {j: lax.ppermute(grads[j], AXES, collect_pairs(j)) for j in (2, 3, 1, 0)}
    backs = [backs[j] for j in range(4)]
    kl = sum(back[ROWS:ROWS + 16].astype(F32) for back in backs)
    kl = jnp.sum(kl.reshape(2, 8, HDIM), axis=0)
    kl = kl + lax.ppermute(kl, AXES, CORE_PAIRS)
    kl = kl + sum(lax.ppermute(kl, AXES, x_pairs(bits)) for bits in (1, 2, 3))
    kl_loss = jnp.sum(kl) / (2.0 * TOKENS * 16)
    half_grad = jax.ShapeDtypeStruct((ROWS, 2 * HDIM), BF16)
    grad_query, grad_key = pl.pallas_call(
        finish_kernel,
        out_shape=[half_grad, half_grad],
        in_specs=[ALL] * 4,
        out_specs=[ALL] * 2,
        scratch_shapes=[pltpu.VMEM((4, ROWS, HDIM), BF16)],
        compiler_params=params(),
    )(*backs)
    return (kl_loss, grad_query, grad_key)


def solution(mesh):
    in_specs = (P("seq", "head"), P("seq", "head"), P("seq", "head"), P("seq", "head"), P("seq"))
    out_specs = (P(), P("seq", "head"), P("seq", "head"))
    return jax.shard_map(
        per_device, mesh=mesh, in_specs=in_specs, out_specs=out_specs, check_vma=False
    )
```

```python
import functools
import math

import jax
import jax.numpy as jnp
from jax import lax
from jax.experimental import pallas as pl
from jax.experimental.pallas import tpu as pltpu
from jax.sharding import PartitionSpec as P

HDIM = 128
TDIM = 256
WIDE = TDIM + HDIM
NY, NZ, NX = 4, 8, 4
ROWS = 128
BLOCK = 512
TILE = 256
TOKENS = 4096
TILES = TOKENS // TILE
NEG = -1e30
LOG2E = 1.4426950408889634
LN2 = 0.6931471805599453
KT = LOG2E / math.sqrt(TDIM)
KS = LOG2E / math.sqrt(HDIM)
VMEM_LIMIT = 48 * 1024 * 1024
ORDER = (0, 1, 3, 2)
PIECE = 2 * ROWS + 16
UNROLL = 2
PACK_FLOPS = 20_000_000_000
F32 = jnp.float32
BF16 = jnp.bfloat16
AXES = ("seq", "head")
ALL = pl.BlockSpec(memory_space=pltpu.VMEM)
ANY = pl.BlockSpec(memory_space=pl.ANY)


def device(y, z, x, core):
    return (y * NZ + z) * (2 * NX) + x * 2 + core


def pairs_of(move):
    pairs = []
    for y in range(NY):
        for z in range(NZ):
            for x in range(NX):
                for core in range(2):
                    pairs.append((device(y, z, x, core), device(*move(y, z, x, core))))
    return pairs


def spread_pairs(j):
    return pairs_of(lambda y, z, x, c: (y, 2 * ((z // 2 + j) % 4) + c, x, z % 2))


def collect_pairs(j):
    return [(target, source) for source, target in spread_pairs(j)]


def near_pairs(sign):
    return pairs_of(lambda y, z, x, c: ((y + sign * (1 - 2 * c)) % NY, z, x, c))


def mirror_pairs(bits):
    return pairs_of(lambda y, z, x, c: (y ^ bits, z, x, c))


def x_pairs(bit):
    return pairs_of(lambda y, z, x, c: (y, z, x ^ bit, c))


CORE_PAIRS = pairs_of(lambda y, z, x, c: (y, z, x, 1 - c))


def placed():
    seq, head = lax.axis_index("seq"), lax.axis_index("head")
    return (lax.div(seq, NZ), lax.rem(seq, NZ), lax.rem(head, 2))


def params(limit=VMEM_LIMIT):
    return pltpu.CompilerParams(vmem_limit_bytes=limit)


def nt_dot(left, right):
    return lax.dot_general(left, right, (((1,), (1,)), ((), ())), preferred_element_type=F32)


def send_kernel(tq, tk, sq, sk, doc, o0, o1, o2, o3, held, docs, sems):
    copies = []
    for m, (teach, pupil) in enumerate(((tq, sq), (tq, sq), (tk, sk), (tk, sk))):
        h = m % 2
        block = held.at[m, pl.ds(0, ROWS)]
        copies.append((teach.at[:, pl.ds(h * TDIM, TDIM)], block.at[:, pl.ds(0, TDIM)]))
        copies.append((pupil.at[:, pl.ds(h * HDIM, HDIM)], block.at[:, pl.ds(TDIM, HDIM)]))
    copies.append((doc, docs))
    copies = [pltpu.make_async_copy(src, dst, sems.at[n]) for n, (src, dst) in enumerate(copies)]
    for copy in reversed(copies):
        copy.start()
    copies.pop().wait()
    below = docs[...] < lax.broadcasted_iota(jnp.int32, (128, ROWS), 0)
    counts = nt_dot(jnp.ones((16, ROWS), BF16), below.astype(F32).astype(BF16))
    for out in (o0, o1, o2, o3):
        out[ROWS:ROWS + 16, 0:128] = counts.astype(BF16)
        out[ROWS:ROWS + 16, 128:WIDE] = jnp.zeros((16, 256), BF16)
    for copy in copies:
        copy.wait()
    b = placed()[1] // 2
    for j, out in enumerate((o0, o1, o2, o3)):
        out[0:ROWS, :] = held[(b + j) % 4]


def pack_kernel(first, second, out):
    out[0:ROWS, :] = first[0:ROWS, :]
    out[ROWS:2 * ROWS, :] = second[0:ROWS, :]
    out[2 * ROWS:PIECE, :] = first[ROWS:ROWS + 16, :] + second[ROWS:ROWS + 16, :]


def pack_both_kernel(before, first, second, out, both):
    pack_kernel(first, second, out)
    both[0:PIECE, :] = before[...]
    both[PIECE:2 * PIECE, :] = out[...]


def group_kernel(*refs):
    out = refs[-1]
    for n, ref in enumerate(refs[:-1]):
        out[n * PIECE:(n + 1) * PIECE, :] = ref[...]


def group(parts):
    return pl.pallas_call(
        group_kernel,
        out_shape=jax.ShapeDtypeStruct((len(parts) * PIECE, WIDE), BF16),
        in_specs=[ALL] * len(parts),
        out_specs=ALL,
        compiler_params=params(),
    )(*parts)


def pieces_of(parts):
    found = []
    for other in range(2):
        own, near_a, far_a, over_a, late, over_b = parts[6 * other:6 * other + 6]
        for part, base, step, chunk in (
            (own, 0, 0, 0),
            (own, 1, 0, 1),
            (near_a, 0, 1, 0),
            (far_a, 0, -1, 0),
            (over_a, 0, 2, 0),
            (late, 0, 1, 1),
            (late, 1, -1, 1),
            (over_b, 0, 2, 1),
        ):
            found.append((part, base * PIECE, step, other, chunk))
    return found


def assemble(parts, rows):
    y, z, core = placed()
    m = z // 2
    total = jnp.zeros((16, 128), F32)
    for part, base, step, other, chunk in pieces_of(parts):
        from_core = core if other == 0 else 1 - core
        from_y = (y - step * (1 - 2 * from_core) + NY) % NY
        for k in range(2):
            b = (m - ORDER[2 * chunk + k] + 4) % 4
            at = (from_y * 8 + 2 * b + from_core) * ROWS
            rows[pl.ds(pl.multiple_of(at, ROWS), ROWS), :] = part[base + k * ROWS:base + (k + 1) * ROWS, :]
        total = total + part[base + 2 * ROWS:base + PIECE, 0:128].astype(F32)
    return total[0:1]


def start_of(bounds, position):
    return jnp.max(jnp.where(bounds <= position, bounds, 0.0))


def end_of(bounds, position):
    return jnp.min(jnp.where(bounds > position, bounds, float(TOKENS)))


def tile_rows(t):
    return pl.ds(pl.multiple_of(t * TILE, TILE), TILE)


def folded(values):
    return values.reshape(TILE // 8, 8, TILE)


def norm_kernel(*refs):
    parts, out = refs[:12], refs[12]
    rows, scores_t, scores_s = refs[13:]
    bounds = assemble(parts, rows)
    y, z, core = placed()
    r = y * 2 + core
    bounds_down = jnp.transpose(jnp.broadcast_to(bounds, (128, 128)))[0:16, 0:1]
    out[...] = jnp.zeros_like(out)
    for half in range(2):
        t = r if half == 0 else TILES - 1 - r
        first = t * TILE
        mine_t = rows[tile_rows(t), 0:TDIM]
        mine_s = rows[tile_rows(t), TDIM:WIDE]
        low = start_of(bounds, first.astype(F32)).astype(jnp.int32)
        high = start_of(bounds, (first + TILE - 1).astype(F32)).astype(jnp.int32)
        my_pos = first + lax.broadcasted_iota(jnp.int32, (1, TILE), 1)
        my_start = jnp.max(
            jnp.where(bounds_down <= my_pos.astype(F32), bounds_down, 0.0), axis=0, keepdims=True
        ).astype(jnp.int32)

        def span(c, n):
            return pl.ds(pl.multiple_of(c * TILE, TILE), n * TILE)

        def eights(values):
            return values.reshape(values.shape[0] // 8, 8, TILE)

        def score(c, tops, n, masked):
            t_tile = nt_dot(rows[span(c, n), 0:TDIM], mine_t) * KT
            s_tile = nt_dot(rows[span(c, n), TDIM:WIDE], mine_s) * KS
            if masked:
                pos = c * TILE + lax.broadcasted_iota(jnp.int32, (n * TILE, TILE), 0)
                seen = (pos <= my_pos) & (pos >= my_start)
                t_tile = jnp.where(seen, t_tile, NEG)
                s_tile = jnp.where(seen, s_tile, NEG)
            scores_t[span(c, n), :] = t_tile
            scores_s[span(c, n), :] = s_tile
            return (
                jnp.maximum(tops[0], jnp.max(eights(t_tile), axis=0)),
                jnp.maximum(tops[1], jnp.max(eights(s_tile), axis=0)),
            )

        def run(begin, stop, carry, body, n=1):
            return lax.fori_loop(0, (stop - begin) // n, lambda i, v: body(begin + n * i, v, n), carry)

        def run_all(begin, stop, carry, body):
            for n in (4, 2, 1):
                middle = stop - (stop - begin) % n
                carry = run(begin, middle, carry, body, n)
                begin = middle
            return carry

        from_tile = low // TILE
        plain_tile = jnp.minimum((high + TILE - 1) // TILE, t)
        tops = (jnp.full((8, TILE), NEG, F32), jnp.full((8, TILE), NEG, F32))
        tops = run_all(from_tile, plain_tile, tops, functools.partial(score, masked=True))
        tops = run_all(plain_tile, t, tops, functools.partial(score, masked=False))
        tops = score(t, tops, 1, True)
        top_t = jnp.max(tops[0], axis=0, keepdims=True)
        top_s = jnp.max(tops[1], axis=0, keepdims=True)

        def add(c, sums, n):
            sum_t, sum_s, cross = sums
            t_tile = scores_t[span(c, n), :]
            s_tile = scores_s[span(c, n), :]
            p = jnp.exp2(t_tile - top_t)
            q = jnp.exp2(s_tile - top_s)
            return (
                sum_t + jnp.sum(eights(p), axis=0),
                sum_s + jnp.sum(eights(q), axis=0),
                cross + jnp.sum(eights(p * (t_tile - s_tile)), axis=0),
            )

        zero = jnp.zeros((8, TILE), F32)
        sums = run_all(from_tile, t + 1, (zero, zero, zero), add)
        sum_t, sum_s, cross = (jnp.sum(v, axis=0, keepdims=True) for v in sums)
        lse_t = top_t * LN2 + jnp.log(sum_t)
        lse_s = top_s * LN2 + jnp.log(sum_s)
        row_kl = cross * LN2 / sum_t - lse_t + lse_s
        for k, lse in enumerate((lse_t, lse_s)):
            high_part = lse.astype(BF16).astype(F32)
            low_part = (lse - high_part).astype(BF16).astype(F32)
            out[2 * half + k:2 * half + k + 1, :] = (high_part + low_part) * LOG2E
        out[4 + half:5 + half, :] = row_kl


def grad_kernel(*refs):
    parts, packets, outs = refs[:12], refs[12:16], refs[16:20]
    rows, norms, row_norm, acc, mine = refs[20:]
    bounds = assemble(parts, rows)
    y, z, core = placed()
    m = z // 2
    kl = jnp.zeros((1, TILE), F32)
    for i, packet in enumerate(packets):
        for other in range(2):
            from_core = core if other == 0 else 1 - core
            from_r = (y ^ i) * 2 + from_core
            norms[from_r, 0:2, :] = packet[8 * other:8 * other + 2, :]
            norms[TILES - 1 - from_r, 0:2, :] = packet[8 * other + 2:8 * other + 4, :]
            kl = kl + packet[8 * other + 4:8 * other + 5, :] + packet[8 * other + 5:8 * other + 6, :]
    kl = kl[:, 0:128] + kl[:, 128:256]
    first = y * (2 * BLOCK) + core * ROWS
    last = first + 7 * ROWS - 1
    for b in range(4):
        sub = slice(b * ROWS, (b + 1) * ROWS)
        mine[sub, :] = rows[pl.ds(pl.multiple_of(first + 2 * b * ROWS, ROWS), ROWS), :]
        for k in range(2):
            line = norms[4 * y + b, k:k + 1, :]
            line = jnp.where(core == 0, line[:, 0:ROWS], line[:, ROWS:TILE])
            row_norm[k, sub] = jnp.transpose(jnp.broadcast_to(line, (ROWS, ROWS)))
    my_index = lax.broadcasted_iota(jnp.int32, (BLOCK, 1), 0)
    my_pos = first + my_index + (my_index // ROWS) * ROWS
    my_posf = my_pos.astype(F32)
    my_start = jnp.max(jnp.where(bounds <= my_posf, bounds, 0.0), axis=1, keepdims=True)
    my_end = jnp.min(jnp.where(bounds > my_posf, bounds, float(TOKENS)), axis=1, keepdims=True)
    my_start, my_end = my_start.astype(jnp.int32), my_end.astype(jnp.int32)
    firstf, lastf = first.astype(F32), last.astype(F32)
    start_low = start_of(bounds, firstf).astype(jnp.int32)
    start_high = start_of(bounds, lastf).astype(jnp.int32)
    end_low = end_of(bounds, firstf).astype(jnp.int32)
    end_high = end_of(bounds, lastf).astype(jnp.int32)
    acc[...] = jnp.zeros_like(acc)

    def columns(c, n):
        return pl.ds(pl.multiple_of(c * TILE, TILE), n * TILE)

    def step(c, n, kind, masked):
        width = n * TILE
        pupil = rows[columns(c, n), TDIM:WIDE]
        t_tile = nt_dot(mine[:, 0:TDIM], rows[columns(c, n), 0:TDIM]) * KT
        s_tile = nt_dot(mine[:, TDIM:WIDE], pupil) * KS
        own_norm = [jnp.concatenate([row_norm[k]] * (2 * n), axis=1) for k in range(2)]
        their_norm = [jnp.concatenate([norms[c + q, k:k + 1, :] for q in range(n)], axis=1) for k in range(2)]
        pos = c * TILE + lax.broadcasted_iota(jnp.int32, (BLOCK, width), 1)
        if kind == "below":
            norm_t, norm_s = own_norm
        elif kind == "above":
            norm_t, norm_s = their_norm
        else:
            own = pos <= my_pos
            norm_t, norm_s = (jnp.where(own, own_norm[k], their_norm[k]) for k in range(2))
        weight = jnp.exp2(s_tile - norm_s) - jnp.exp2(t_tile - norm_t)
        if kind == "diagonal":
            weight = jnp.where(pos == my_pos, 2.0 * weight, weight)
        if masked:
            weight = jnp.where((pos >= my_start) & (pos < my_end), weight, 0.0)
        acc[...] += jnp.dot(weight.astype(BF16), pupil, preferred_element_type=F32)

    def run(begin, stop, kind, masked, n=1):
        def body(i, unused):
            step(begin + n * i, n, kind, masked)
            return unused

        lax.fori_loop(0, (stop - begin) // n, body, 0)

    diag = 4 * y
    plain = jnp.minimum((start_high + TILE - 1) // TILE, diag)
    begin = start_low // TILE
    odd = plain - (plain - begin) % UNROLL
    run(begin, odd, "below", True, UNROLL)
    run(odd, plain, "below", True)
    odd = plain + (diag - plain) % UNROLL
    run(plain, odd, "below", False)
    run(odd, diag, "below", False, UNROLL)
    run(diag, diag + 4, "diagonal", True, 2)
    plain = jnp.maximum(end_low // TILE, diag + 4)
    odd = diag + 4 + (plain - diag - 4) % UNROLL
    run(diag + 4, odd, "above", False)
    run(odd, plain, "above", False, UNROLL)
    stop = (end_high + TILE - 1) // TILE
    odd = plain + (stop - plain) % UNROLL
    run(plain, odd, "above", True)
    run(odd, stop, "above", True, UNROLL)
    for b in range(4):
        for j in range(4):

            @pl.when((m - j + 4) % 4 == b)
            def _():
                outs[j][0:ROWS, :] = acc[b * ROWS:(b + 1) * ROWS, :].astype(BF16)

    high_part = kl.astype(BF16).astype(F32)
    mid_part = (kl - high_part).astype(BF16).astype(F32)
    low_part = (kl - high_part - mid_part).astype(BF16).astype(F32)
    line = lax.broadcasted_iota(jnp.int32, (16, 128), 0)
    tail = jnp.where(line == 0, high_part, jnp.where(line == 1, mid_part, jnp.where(line == 2, low_part, 0.0)))
    for j in range(4):
        outs[j][ROWS:ROWS + 16, :] = tail.astype(BF16)


def finish_kernel(g0, g1, g2, g3, grad_q, grad_k, held):
    b = placed()[1] // 2
    for j, got in enumerate((g0, g1, g2, g3)):
        held[(b + j) % 4] = got[0:ROWS, :]
    for m in range(4):
        out = grad_q if m < 2 else grad_k
        h = m % 2
        out[:, h * HDIM:(h + 1) * HDIM] = held[m]


def call_norm(parts):
    return pl.pallas_call(
        norm_kernel,
        out_shape=jax.ShapeDtypeStruct((8, TILE), F32),
        in_specs=[ALL] * 12,
        out_specs=ALL,
        scratch_shapes=[
            pltpu.VMEM((TOKENS, WIDE), BF16),
            pltpu.VMEM((TOKENS, TILE), F32),
            pltpu.VMEM((TOKENS, TILE), F32),
        ],
        compiler_params=params(),
    )(*parts)


def call_grad(parts, packets):
    return pl.pallas_call(
        grad_kernel,
        out_shape=[jax.ShapeDtypeStruct((ROWS + 16, HDIM), BF16)] * 4,
        in_specs=[ALL] * 16,
        out_specs=[ALL] * 4,
        scratch_shapes=[
            pltpu.VMEM((TOKENS, WIDE), BF16),
            pltpu.VMEM((TILES, 8, TILE), F32),
            pltpu.VMEM((2, BLOCK, 128), F32),
            pltpu.VMEM((BLOCK, HDIM), F32),
            pltpu.VMEM((BLOCK, WIDE), BF16),
        ],
        compiler_params=params(),
    )(*parts, *packets)


def per_device(teacher_query, teacher_key, student_query, student_key, doc_ids):
    block = jax.ShapeDtypeStruct((ROWS + 16, WIDE), BF16)
    sends = pl.pallas_call(
        send_kernel,
        out_shape=[block] * 4,
        in_specs=[ANY] * 5,
        out_specs=[ALL] * 4,
        scratch_shapes=[
            pltpu.VMEM((4, ROWS, WIDE), BF16),
            pltpu.VMEM((1, ROWS), jnp.int32),
            pltpu.SemaphoreType.DMA((9,)),
        ],
        compiler_params=params(60 * 1024 * 1024),
    )(teacher_query, teacher_key, student_query, student_key, doc_ids.reshape(1, ROWS))
    gots = [lax.ppermute(sends[j], AXES, spread_pairs(j)) for j in ORDER]
    piece = jax.ShapeDtypeStruct((PIECE, WIDE), BF16)
    own_a = pl.pallas_call(
        pack_kernel,
        out_shape=piece,
        in_specs=[ALL] * 2,
        out_specs=ALL,
        compiler_params=params(),
        cost_estimate=pl.CostEstimate(
            flops=PACK_FLOPS, bytes_accessed=4 * PIECE * WIDE, transcendentals=0
        ),
    )(*gots[0:2])
    own_b, own = pl.pallas_call(
        pack_both_kernel,
        out_shape=[piece, jax.ShapeDtypeStruct((2 * PIECE, WIDE), BF16)],
        in_specs=[ALL] * 3,
        out_specs=[ALL] * 2,
        compiler_params=params(),
    )(own_a, *gots[2:4])
    near_a, near_b = (lax.ppermute(mine, AXES, near_pairs(1)) for mine in (own_a, own_b))
    far_a, far_b = (lax.ppermute(mine, AXES, near_pairs(-1)) for mine in (own_a, own_b))
    over_a, over_b = (lax.ppermute(near, AXES, near_pairs(1)) for near in (near_a, near_b))
    parts = [own, near_a, far_a, over_a, group([near_b, far_b]), over_b]
    parts += [lax.ppermute(part, AXES, CORE_PAIRS) for part in parts]
    packet = call_norm(parts)
    both = jnp.concatenate([packet, lax.ppermute(packet, AXES, CORE_PAIRS)])
    others = {step: lax.ppermute(both, AXES, mirror_pairs(step)) for step in (2, 1, 3)}
    packets = [both] + [others[step] for step in (1, 2, 3)]
    grads = call_grad(parts, packets)
    backs = {j: lax.ppermute(grads[j], AXES, collect_pairs(j)) for j in (2, 3, 1, 0)}
    backs = [backs[j] for j in range(4)]
    kl = sum(back[ROWS:ROWS + 16].astype(F32) for back in backs)
    kl = jnp.sum(kl.reshape(2, 8, HDIM), axis=0)
    kl = kl + lax.ppermute(kl, AXES, CORE_PAIRS)
    kl = kl + sum(lax.ppermute(kl, AXES, x_pairs(bits)) for bits in (1, 2, 3))
    kl_loss = jnp.sum(kl) / (2.0 * TOKENS * 16)
    half_grad = jax.ShapeDtypeStruct((ROWS, 2 * HDIM), BF16)
    grad_query, grad_key = pl.pallas_call(
        finish_kernel,
        out_shape=[half_grad, half_grad],
        in_specs=[ALL] * 4,
        out_specs=[ALL] * 2,
        scratch_shapes=[pltpu.VMEM((4, ROWS, HDIM), BF16)],
        compiler_params=params(),
    )(*backs)
    return (kl_loss, grad_query, grad_key)


def solution(mesh):
    in_specs = (P("seq", "head"), P("seq", "head"), P("seq", "head"), P("seq", "head"), P("seq"))
    out_specs = (P(), P("seq", "head"), P("seq", "head"))
    return jax.shard_map(
        per_device, mesh=mesh, in_specs=in_specs, out_specs=out_specs, check_vma=False
    )
```

```python
import functools
import math

import jax
import jax.numpy as jnp
from jax import lax
from jax.experimental import pallas as pl
from jax.experimental.pallas import tpu as pltpu
from jax.sharding import PartitionSpec as P

HDIM = 128
TDIM = 256
WIDE = TDIM + HDIM
NY, NZ, NX = 4, 8, 4
ROWS = 128
BLOCK = 512
TILE = 256
TOKENS = 4096
TILES = TOKENS // TILE
NEG = -1e30
LOG2E = 1.4426950408889634
LN2 = 0.6931471805599453
KT = LOG2E / math.sqrt(TDIM)
KS = LOG2E / math.sqrt(HDIM)
VMEM_LIMIT = 48 * 1024 * 1024
ORDER = (0, 1, 3, 2)
PIECE = 2 * ROWS + 16
UNROLL = 2
STEP = 1
SPANS = (4, 2, 1)
PACK_FLOPS = 20_000_000_000
F32 = jnp.float32
BF16 = jnp.bfloat16
AXES = ("seq", "head")
ALL = pl.BlockSpec(memory_space=pltpu.VMEM)
ANY = pl.BlockSpec(memory_space=pl.ANY)


def device(y, z, x, core):
    return (y * NZ + z) * (2 * NX) + x * 2 + core


def pairs_of(move):
    pairs = []
    for y in range(NY):
        for z in range(NZ):
            for x in range(NX):
                for core in range(2):
                    pairs.append((device(y, z, x, core), device(*move(y, z, x, core))))
    return pairs


def spread_pairs(j):
    return pairs_of(lambda y, z, x, c: (y, 2 * ((z // 2 + j) % 4) + c, x, z % 2))


def collect_pairs(j):
    return [(target, source) for source, target in spread_pairs(j)]


def near_pairs(sign):
    return pairs_of(lambda y, z, x, c: ((y + sign * (1 - 2 * c)) % NY, z, x, c))


def mirror_pairs(bits):
    return pairs_of(lambda y, z, x, c: (y ^ bits, z, x, c))


def x_pairs(bit):
    return pairs_of(lambda y, z, x, c: (y, z, x ^ bit, c))


CORE_PAIRS = pairs_of(lambda y, z, x, c: (y, z, x, 1 - c))


def placed():
    seq, head = lax.axis_index("seq"), lax.axis_index("head")
    return (lax.div(seq, NZ), lax.rem(seq, NZ), lax.rem(head, 2))


def params(limit=VMEM_LIMIT):
    return pltpu.CompilerParams(vmem_limit_bytes=limit)


def nt_dot(left, right):
    return lax.dot_general(left, right, (((1,), (1,)), ((), ())), preferred_element_type=F32)


def send_kernel(tq, tk, sq, sk, doc, o0, o1, o2, o3, held, docs, sems):
    copies = []
    for m, (teach, pupil) in enumerate(((tq, sq), (tq, sq), (tk, sk), (tk, sk))):
        h = m % 2
        block = held.at[m, pl.ds(0, ROWS)]
        copies.append((teach.at[:, pl.ds(h * TDIM, TDIM)], block.at[:, pl.ds(0, TDIM)]))
        copies.append((pupil.at[:, pl.ds(h * HDIM, HDIM)], block.at[:, pl.ds(TDIM, HDIM)]))
    copies.append((doc, docs))
    copies = [pltpu.make_async_copy(src, dst, sems.at[n]) for n, (src, dst) in enumerate(copies)]
    for copy in reversed(copies):
        copy.start()
    copies.pop().wait()
    below = docs[...] < lax.broadcasted_iota(jnp.int32, (128, ROWS), 0)
    counts = nt_dot(jnp.ones((16, ROWS), BF16), below.astype(F32).astype(BF16))
    for out in (o0, o1, o2, o3):
        out[ROWS:ROWS + 16, 0:128] = counts.astype(BF16)
        out[ROWS:ROWS + 16, 128:WIDE] = jnp.zeros((16, 256), BF16)
    for copy in copies:
        copy.wait()
    b = placed()[1] // 2
    for j, out in enumerate((o0, o1, o2, o3)):
        out[0:ROWS, :] = held[(b + j) % 4]


def pack_kernel(first, second, out):
    out[0:ROWS, :] = first[0:ROWS, :]
    out[ROWS:2 * ROWS, :] = second[0:ROWS, :]
    out[2 * ROWS:PIECE, :] = first[ROWS:ROWS + 16, :] + second[ROWS:ROWS + 16, :]


def pack_both_kernel(before, first, second, out, both):
    pack_kernel(first, second, out)
    both[0:PIECE, :] = before[...]
    both[PIECE:2 * PIECE, :] = out[...]


def group_kernel(*refs):
    out = refs[-1]
    for n, ref in enumerate(refs[:-1]):
        out[n * PIECE:(n + 1) * PIECE, :] = ref[...]


def group(parts):
    return pl.pallas_call(
        group_kernel,
        out_shape=jax.ShapeDtypeStruct((len(parts) * PIECE, WIDE), BF16),
        in_specs=[ALL] * len(parts),
        out_specs=ALL,
        compiler_params=params(),
    )(*parts)


def pieces_of(parts):
    found = []
    for other in range(2):
        own, near_a, far_a, over_a, late, over_b = parts[6 * other:6 * other + 6]
        for part, base, step, chunk in (
            (own, 0, 0, 0),
            (own, 1, 0, 1),
            (near_a, 0, 1, 0),
            (far_a, 0, -1, 0),
            (over_a, 0, 2, 0),
            (late, 0, 1, 1),
            (late, 1, -1, 1),
            (over_b, 0, 2, 1),
        ):
            found.append((part, base * PIECE, step, other, chunk))
    return found


def assemble(parts, rows):
    y, z, core = placed()
    m = z // 2
    total = jnp.zeros((16, 128), F32)
    for part, base, step, other, chunk in pieces_of(parts):
        from_core = core if other == 0 else 1 - core
        from_y = (y - step * (1 - 2 * from_core) + NY) % NY
        for k in range(2):
            b = (m - ORDER[2 * chunk + k] + 4) % 4
            at = (from_y * 8 + 2 * b + from_core) * ROWS
            rows[pl.ds(pl.multiple_of(at, ROWS), ROWS), :] = part[base + k * ROWS:base + (k + 1) * ROWS, :]
        total = total + part[base + 2 * ROWS:base + PIECE, 0:128].astype(F32)
    return total[0:1]


def start_of(bounds, position):
    return jnp.max(jnp.where(bounds <= position, bounds, 0.0))


def end_of(bounds, position):
    return jnp.min(jnp.where(bounds > position, bounds, float(TOKENS)))


def tile_rows(t):
    return pl.ds(pl.multiple_of(t * TILE, TILE), TILE)


def bounds_in_rows(bounds):
    return jnp.transpose(jnp.broadcast_to(bounds, (128, 128)))[0:16, 0:1]


def eights(values):
    return values.reshape(values.shape[0] // 8, 8, TILE)


def norm_kernel(*refs):
    parts, out, rows = refs[:12], refs[12], refs[13]
    bounds = assemble(parts, rows)
    y, z, core = placed()
    r = y * 2 + core
    bounds_down = bounds_in_rows(bounds)
    out[...] = jnp.zeros_like(out)
    for half in range(2):
        t = r if half == 0 else TILES - 1 - r
        first = t * TILE
        low = start_of(bounds, first.astype(F32)).astype(jnp.int32)
        high = start_of(bounds, (first + TILE - 1).astype(F32)).astype(jnp.int32)
        my_pos = first + lax.broadcasted_iota(jnp.int32, (1, TILE), 1)
        my_start = jnp.max(
            jnp.where(bounds_down <= my_pos.astype(F32), bounds_down, 0.0), axis=0, keepdims=True
        ).astype(jnp.int32)

        def online(c, state, n, masked):
            top_t, top_s, sum_t, sum_s, cross = state
            span = pl.ds(pl.multiple_of(c * TILE, TILE), n * TILE)
            t_tile = nt_dot(rows[span, 0:TDIM], rows[tile_rows(t), 0:TDIM]) * KT
            s_tile = nt_dot(rows[span, TDIM:WIDE], rows[tile_rows(t), TDIM:WIDE]) * KS
            if masked:
                pos = c * TILE + lax.broadcasted_iota(jnp.int32, (n * TILE, TILE), 0)
                seen = (pos <= my_pos) & (pos >= my_start)
                t_tile = jnp.where(seen, t_tile, NEG)
                s_tile = jnp.where(seen, s_tile, NEG)
            new_t = jnp.maximum(top_t, jnp.max(jnp.max(eights(t_tile), axis=0), axis=0, keepdims=True))
            new_s = jnp.maximum(top_s, jnp.max(jnp.max(eights(s_tile), axis=0), axis=0, keepdims=True))
            p = jnp.exp2(t_tile - new_t)
            q = jnp.exp2(s_tile - new_s)
            decay_t = jnp.exp2(top_t - new_t)
            decay_s = jnp.exp2(top_s - new_s)
            return (
                new_t,
                new_s,
                sum_t * decay_t + jnp.sum(eights(p), axis=0),
                sum_s * decay_s + jnp.sum(eights(q), axis=0),
                cross * decay_t + jnp.sum(eights(p * (t_tile - s_tile)), axis=0),
            )

        def several(c, state, n, masked):
            for part in range(0, n, STEP):
                state = online(c + part, state, min(n, STEP), masked)
            return state

        def run_all(begin, stop, state, masked):
            for n in SPANS:
                middle = stop - (stop - begin) % n
                state = lax.fori_loop(
                    0,
                    (middle - begin) // n,
                    lambda i, v: several(begin + n * i, v, n, masked),
                    state,
                )
                begin = middle
            return state

        from_tile = low // TILE
        plain_tile = jnp.minimum((high + TILE - 1) // TILE, t)
        none, zero = jnp.full((1, TILE), NEG, F32), jnp.zeros((8, TILE), F32)
        state = online(t, (none, none, zero, zero, zero), 1, True)
        state = run_all(from_tile, plain_tile, state, True)
        state = run_all(plain_tile, t, state, False)
        top_t, top_s = state[:2]
        sum_t, sum_s, cross = (jnp.sum(v, axis=0, keepdims=True) for v in state[2:])
        lse_t = top_t * LN2 + jnp.log(sum_t)
        lse_s = top_s * LN2 + jnp.log(sum_s)
        row_kl = cross * LN2 / sum_t - lse_t + lse_s
        for k, lse in enumerate((lse_t, lse_s)):
            high_part = lse.astype(BF16).astype(F32)
            low_part = (lse - high_part).astype(BF16).astype(F32)
            out[2 * half + k:2 * half + k + 1, :] = (high_part + low_part) * LOG2E
        out[4 + half:5 + half, :] = row_kl


def grad_kernel(*refs):
    parts, packets, outs = refs[:12], refs[12:16], refs[16:20]
    rows, norms, row_norm, acc, mine = refs[20:]
    bounds = assemble(parts, rows)
    y, z, core = placed()
    m = z // 2
    kl = jnp.zeros((1, TILE), F32)
    for i, packet in enumerate(packets):
        for other in range(2):
            from_core = core if other == 0 else 1 - core
            from_r = (y ^ i) * 2 + from_core
            norms[from_r, 0:2, :] = packet[8 * other:8 * other + 2, :]
            norms[TILES - 1 - from_r, 0:2, :] = packet[8 * other + 2:8 * other + 4, :]
            kl = kl + packet[8 * other + 4:8 * other + 5, :] + packet[8 * other + 5:8 * other + 6, :]
    kl = kl[:, 0:128] + kl[:, 128:256]
    first = y * (2 * BLOCK) + core * ROWS
    last = first + 7 * ROWS - 1
    for b in range(4):
        sub = slice(b * ROWS, (b + 1) * ROWS)
        mine[sub, :] = rows[pl.ds(pl.multiple_of(first + 2 * b * ROWS, ROWS), ROWS), :]
        for k in range(2):
            line = norms[4 * y + b, k:k + 1, :]
            line = jnp.where(core == 0, line[:, 0:ROWS], line[:, ROWS:TILE])
            row_norm[k, sub] = jnp.transpose(jnp.broadcast_to(line, (ROWS, ROWS)))
    my_index = lax.broadcasted_iota(jnp.int32, (BLOCK, 1), 0)
    my_pos = first + my_index + (my_index // ROWS) * ROWS
    my_posf = my_pos.astype(F32)
    my_start = jnp.max(jnp.where(bounds <= my_posf, bounds, 0.0), axis=1, keepdims=True)
    my_end = jnp.min(jnp.where(bounds > my_posf, bounds, float(TOKENS)), axis=1, keepdims=True)
    my_start, my_end = my_start.astype(jnp.int32), my_end.astype(jnp.int32)
    firstf, lastf = first.astype(F32), last.astype(F32)
    start_low = start_of(bounds, firstf).astype(jnp.int32)
    start_high = start_of(bounds, lastf).astype(jnp.int32)
    end_low = end_of(bounds, firstf).astype(jnp.int32)
    end_high = end_of(bounds, lastf).astype(jnp.int32)
    acc[...] = jnp.zeros_like(acc)

    def columns(c, n):
        return pl.ds(pl.multiple_of(c * TILE, TILE), n * TILE)

    def step(c, n, kind, masked):
        width = n * TILE
        pupil = rows[columns(c, n), TDIM:WIDE]
        t_tile = nt_dot(mine[:, 0:TDIM], rows[columns(c, n), 0:TDIM]) * KT
        s_tile = nt_dot(mine[:, TDIM:WIDE], pupil) * KS
        own_norm = [jnp.concatenate([row_norm[k]] * (2 * n), axis=1) for k in range(2)]
        their_norm = [jnp.concatenate([norms[c + q, k:k + 1, :] for q in range(n)], axis=1) for k in range(2)]
        pos = c * TILE + lax.broadcasted_iota(jnp.int32, (BLOCK, width), 1)
        if kind == "below":
            norm_t, norm_s = own_norm
        elif kind == "above":
            norm_t, norm_s = their_norm
        else:
            own = pos <= my_pos
            norm_t, norm_s = (jnp.where(own, own_norm[k], their_norm[k]) for k in range(2))
        weight = jnp.exp2(s_tile - norm_s) - jnp.exp2(t_tile - norm_t)
        if kind == "diagonal":
            weight = jnp.where(pos == my_pos, 2.0 * weight, weight)
        if masked:
            weight = jnp.where((pos >= my_start) & (pos < my_end), weight, 0.0)
        acc[...] += jnp.dot(weight.astype(BF16), pupil, preferred_element_type=F32)

    def run(begin, stop, kind, masked, n=1):
        def body(i, unused):
            step(begin + n * i, n, kind, masked)
            return unused

        lax.fori_loop(0, (stop - begin) // n, body, 0)

    wide = UNROLL * TILE
    diag = 4 * y
    plain = jnp.minimum((start_high + wide - 1) // wide * UNROLL, diag)
    run(start_low // wide * UNROLL, plain, "below", True, UNROLL)
    run(plain, diag, "below", False, UNROLL)
    run(diag, diag + 4, "diagonal", True, UNROLL)
    plain = jnp.maximum(end_low // wide * UNROLL, diag + 4)
    run(diag + 4, plain, "above", False, UNROLL)
    run(plain, (end_high + wide - 1) // wide * UNROLL, "above", True, UNROLL)
    for b in range(4):
        for j in range(4):

            @pl.when((m - j + 4) % 4 == b)
            def _():
                outs[j][0:ROWS, :] = acc[b * ROWS:(b + 1) * ROWS, :].astype(BF16)

    high_part = kl.astype(BF16).astype(F32)
    mid_part = (kl - high_part).astype(BF16).astype(F32)
    low_part = (kl - high_part - mid_part).astype(BF16).astype(F32)
    line = lax.broadcasted_iota(jnp.int32, (16, 128), 0)
    tail = jnp.where(line == 0, high_part, jnp.where(line == 1, mid_part, jnp.where(line == 2, low_part, 0.0)))
    for j in range(4):
        outs[j][ROWS:ROWS + 16, :] = tail.astype(BF16)


def finish_kernel(g0, g1, g2, g3, grad_q, grad_k, held):
    b = placed()[1] // 2
    for j, got in enumerate((g0, g1, g2, g3)):
        held[(b + j) % 4] = got[0:ROWS, :]
    for m in range(4):
        out = grad_q if m < 2 else grad_k
        h = m % 2
        out[:, h * HDIM:(h + 1) * HDIM] = held[m]


def call_norm(parts):
    return pl.pallas_call(
        norm_kernel,
        out_shape=jax.ShapeDtypeStruct((8, TILE), F32),
        in_specs=[ALL] * 12,
        out_specs=ALL,
        scratch_shapes=[
            pltpu.VMEM((TOKENS, WIDE), BF16),
        ],
        compiler_params=params(),
    )(*parts)


def call_grad(parts, packets):
    return pl.pallas_call(
        grad_kernel,
        out_shape=[jax.ShapeDtypeStruct((ROWS + 16, HDIM), BF16)] * 4,
        in_specs=[ALL] * 16,
        out_specs=[ALL] * 4,
        scratch_shapes=[
            pltpu.VMEM((TOKENS, WIDE), BF16),
            pltpu.VMEM((TILES, 8, TILE), F32),
            pltpu.VMEM((2, BLOCK, 128), F32),
            pltpu.VMEM((BLOCK, HDIM), F32),
            pltpu.VMEM((BLOCK, WIDE), BF16),
        ],
        compiler_params=params(),
    )(*parts, *packets)


def per_device(teacher_query, teacher_key, student_query, student_key, doc_ids):
    block = jax.ShapeDtypeStruct((ROWS + 16, WIDE), BF16)
    sends = pl.pallas_call(
        send_kernel,
        out_shape=[block] * 4,
        in_specs=[ANY] * 5,
        out_specs=[ALL] * 4,
        scratch_shapes=[
            pltpu.VMEM((4, ROWS, WIDE), BF16),
            pltpu.VMEM((1, ROWS), jnp.int32),
            pltpu.SemaphoreType.DMA((9,)),
        ],
        compiler_params=params(60 * 1024 * 1024),
    )(teacher_query, teacher_key, student_query, student_key, doc_ids.reshape(1, ROWS))
    gots = [lax.ppermute(sends[j], AXES, spread_pairs(j)) for j in ORDER]
    piece = jax.ShapeDtypeStruct((PIECE, WIDE), BF16)
    own_a = pl.pallas_call(
        pack_kernel,
        out_shape=piece,
        in_specs=[ALL] * 2,
        out_specs=ALL,
        compiler_params=params(),
        cost_estimate=pl.CostEstimate(
            flops=PACK_FLOPS, bytes_accessed=4 * PIECE * WIDE, transcendentals=0
        ),
    )(*gots[0:2])
    own_b, own = pl.pallas_call(
        pack_both_kernel,
        out_shape=[piece, jax.ShapeDtypeStruct((2 * PIECE, WIDE), BF16)],
        in_specs=[ALL] * 3,
        out_specs=[ALL] * 2,
        compiler_params=params(),
    )(own_a, *gots[2:4])
    near_a, near_b = (lax.ppermute(mine, AXES, near_pairs(1)) for mine in (own_a, own_b))
    far_a, far_b = (lax.ppermute(mine, AXES, near_pairs(-1)) for mine in (own_a, own_b))
    over_a, over_b = (lax.ppermute(near, AXES, near_pairs(1)) for near in (near_a, near_b))
    parts = [own, near_a, far_a, over_a, group([near_b, far_b]), over_b]
    parts += [lax.ppermute(part, AXES, CORE_PAIRS) for part in parts]
    packet = call_norm(parts)
    both = jnp.concatenate([packet, lax.ppermute(packet, AXES, CORE_PAIRS)])
    others = {step: lax.ppermute(both, AXES, mirror_pairs(step)) for step in (3, 1, 2)}
    packets = [both] + [others[step] for step in (1, 2, 3)]
    grads = call_grad(parts, packets)
    backs = {j: lax.ppermute(grads[j], AXES, collect_pairs(j)) for j in (2, 3, 1, 0)}
    backs = [backs[j] for j in range(4)]
    kl = sum(back[ROWS:ROWS + 16].astype(F32) for back in backs)
    kl = jnp.sum(kl.reshape(2, 8, HDIM), axis=0)
    kl = kl + lax.ppermute(kl, AXES, CORE_PAIRS)
    kl = kl + sum(lax.ppermute(kl, AXES, x_pairs(bits)) for bits in (1, 2, 3))
    kl_loss = jnp.sum(kl) / (2.0 * TOKENS * 16)
    half_grad = jax.ShapeDtypeStruct((ROWS, 2 * HDIM), BF16)
    grad_query, grad_key = pl.pallas_call(
        finish_kernel,
        out_shape=[half_grad, half_grad],
        in_specs=[ALL] * 4,
        out_specs=[ALL] * 2,
        scratch_shapes=[pltpu.VMEM((4, ROWS, HDIM), BF16)],
        compiler_params=params(),
    )(*backs)
    return (kl_loss, grad_query, grad_key)


def solution(mesh):
    in_specs = (P("seq", "head"), P("seq", "head"), P("seq", "head"), P("seq", "head"), P("seq"))
    out_specs = (P(), P("seq", "head"), P("seq", "head"))
    return jax.shard_map(
        per_device, mesh=mesh, in_specs=in_specs, out_specs=out_specs, check_vma=False
    )
```

```python
import functools
import math

import jax
import jax.numpy as jnp
from jax import lax
from jax.experimental import pallas as pl
from jax.experimental.pallas import tpu as pltpu
from jax.sharding import PartitionSpec as P

HDIM = 128
TDIM = 256
WIDE = TDIM + HDIM
NY, NZ, NX = 4, 8, 4
ROWS = 128
BLOCK = 512
TILE = 256
TOKENS = 4096
TILES = TOKENS // TILE
NEG = -1e30
LOG2E = 1.4426950408889634
LN2 = 0.6931471805599453
KT = LOG2E / math.sqrt(TDIM)
KS = LOG2E / math.sqrt(HDIM)
VMEM_LIMIT = 48 * 1024 * 1024
ORDER = (0, 1, 3, 2)
PIECE = 2 * ROWS + 16
UNROLL = 2
PACK_FLOPS = 20_000_000_000
F32 = jnp.float32
BF16 = jnp.bfloat16
AXES = ("seq", "head")
ALL = pl.BlockSpec(memory_space=pltpu.VMEM)
ANY = pl.BlockSpec(memory_space=pl.ANY)


def device(y, z, x, core):
    return (y * NZ + z) * (2 * NX) + x * 2 + core


def pairs_of(move):
    pairs = []
    for y in range(NY):
        for z in range(NZ):
            for x in range(NX):
                for core in range(2):
                    pairs.append((device(y, z, x, core), device(*move(y, z, x, core))))
    return pairs


def spread_pairs(j):
    return pairs_of(lambda y, z, x, c: (y, 2 * ((z // 2 + j) % 4) + c, x, z % 2))


def collect_pairs(j):
    return [(target, source) for source, target in spread_pairs(j)]


def near_pairs(sign):
    return pairs_of(lambda y, z, x, c: ((y + sign * (1 - 2 * c)) % NY, z, x, c))


def mirror_pairs(bits):
    return pairs_of(lambda y, z, x, c: (y ^ bits, z, x, c))


def x_pairs(bit):
    return pairs_of(lambda y, z, x, c: (y, z, x ^ bit, c))


CORE_PAIRS = pairs_of(lambda y, z, x, c: (y, z, x, 1 - c))


def placed():
    seq, head = lax.axis_index("seq"), lax.axis_index("head")
    return (lax.div(seq, NZ), lax.rem(seq, NZ), lax.rem(head, 2))


def params(limit=VMEM_LIMIT):
    return pltpu.CompilerParams(vmem_limit_bytes=limit)


def nt_dot(left, right):
    return lax.dot_general(left, right, (((1,), (1,)), ((), ())), preferred_element_type=F32)


def send_kernel(tq, tk, sq, sk, doc, o0, o1, o2, o3, held, docs, sems):
    copies = []
    for m, (teach, pupil) in enumerate(((tq, sq), (tq, sq), (tk, sk), (tk, sk))):
        h = m % 2
        block = held.at[m, pl.ds(0, ROWS)]
        copies.append((teach.at[:, pl.ds(h * TDIM, TDIM)], block.at[:, pl.ds(0, TDIM)]))
        copies.append((pupil.at[:, pl.ds(h * HDIM, HDIM)], block.at[:, pl.ds(TDIM, HDIM)]))
    copies.append((doc, docs))
    copies = [pltpu.make_async_copy(src, dst, sems.at[n]) for n, (src, dst) in enumerate(copies)]
    for copy in reversed(copies):
        copy.start()
    copies.pop().wait()
    below = docs[...] < lax.broadcasted_iota(jnp.int32, (128, ROWS), 0)
    counts = nt_dot(jnp.ones((16, ROWS), BF16), below.astype(F32).astype(BF16))
    for out in (o0, o1, o2, o3):
        out[ROWS:ROWS + 16, 0:128] = counts.astype(BF16)
        out[ROWS:ROWS + 16, 128:WIDE] = jnp.zeros((16, 256), BF16)
    for copy in copies:
        copy.wait()
    b = placed()[1] // 2
    for j, out in enumerate((o0, o1, o2, o3)):
        out[0:ROWS, :] = held[(b + j) % 4]


def pack_kernel(first, second, out):
    out[0:ROWS, :] = first[0:ROWS, :]
    out[ROWS:2 * ROWS, :] = second[0:ROWS, :]
    out[2 * ROWS:PIECE, :] = first[ROWS:ROWS + 16, :] + second[ROWS:ROWS + 16, :]


def pack_both_kernel(before, first, second, out, both):
    pack_kernel(first, second, out)
    both[0:PIECE, :] = before[...]
    both[PIECE:2 * PIECE, :] = out[...]


def group_kernel(*refs):
    out = refs[-1]
    for n, ref in enumerate(refs[:-1]):
        out[n * PIECE:(n + 1) * PIECE, :] = ref[...]


def group(parts):
    return pl.pallas_call(
        group_kernel,
        out_shape=jax.ShapeDtypeStruct((len(parts) * PIECE, WIDE), BF16),
        in_specs=[ALL] * len(parts),
        out_specs=ALL,
        compiler_params=params(),
    )(*parts)


def pieces_of(parts):
    found = []
    for other in range(2):
        own, near_a, far_a, over_a, late, over_b = parts[6 * other:6 * other + 6]
        for part, base, step, chunk in (
            (own, 0, 0, 0),
            (own, 1, 0, 1),
            (near_a, 0, 1, 0),
            (far_a, 0, -1, 0),
            (over_a, 0, 2, 0),
            (late, 0, 1, 1),
            (late, 1, -1, 1),
            (over_b, 0, 2, 1),
        ):
            found.append((part, base * PIECE, step, other, chunk))
    return found


def assemble(parts, rows):
    y, z, core = placed()
    m = z // 2
    total = jnp.zeros((16, 128), F32)
    for part, base, step, other, chunk in pieces_of(parts):
        from_core = core if other == 0 else 1 - core
        from_y = (y - step * (1 - 2 * from_core) + NY) % NY
        for k in range(2):
            b = (m - ORDER[2 * chunk + k] + 4) % 4
            at = (from_y * 8 + 2 * b + from_core) * ROWS
            rows[pl.ds(pl.multiple_of(at, ROWS), ROWS), :] = part[base + k * ROWS:base + (k + 1) * ROWS, :]
        total = total + part[base + 2 * ROWS:base + PIECE, 0:128].astype(F32)
    return total[0:1]


def start_of(bounds, position):
    return jnp.max(jnp.where(bounds <= position, bounds, 0.0))


def end_of(bounds, position):
    return jnp.min(jnp.where(bounds > position, bounds, float(TOKENS)))


def tile_rows(t):
    return pl.ds(pl.multiple_of(t * TILE, TILE), TILE)


def folded(values):
    return values.reshape(TILE // 8, 8, TILE)


def norm_kernel(*refs):
    parts, out = refs[:12], refs[12]
    rows, scores_t, scores_s = refs[13:]
    bounds = assemble(parts, rows)
    y, z, core = placed()
    r = y * 2 + core
    bounds_down = jnp.transpose(jnp.broadcast_to(bounds, (128, 128)))[0:16, 0:1]
    out[...] = jnp.zeros_like(out)
    for half in range(2):
        t = r if half == 0 else TILES - 1 - r
        first = t * TILE
        mine_t = rows[tile_rows(t), 0:TDIM]
        mine_s = rows[tile_rows(t), TDIM:WIDE]
        low = start_of(bounds, first.astype(F32)).astype(jnp.int32)
        high = start_of(bounds, (first + TILE - 1).astype(F32)).astype(jnp.int32)
        my_pos = first + lax.broadcasted_iota(jnp.int32, (1, TILE), 1)
        my_start = jnp.max(
            jnp.where(bounds_down <= my_pos.astype(F32), bounds_down, 0.0), axis=0, keepdims=True
        ).astype(jnp.int32)

        def span(c, n):
            return pl.ds(pl.multiple_of(c * TILE, TILE), n * TILE)

        def eights(values):
            return values.reshape(values.shape[0] // 8, 8, TILE)

        def score(c, tops, n, masked):
            t_tile = nt_dot(rows[span(c, n), 0:TDIM], mine_t) * KT
            s_tile = nt_dot(rows[span(c, n), TDIM:WIDE], mine_s) * KS
            if masked:
                pos = c * TILE + lax.broadcasted_iota(jnp.int32, (n * TILE, TILE), 0)
                seen = (pos <= my_pos) & (pos >= my_start)
                t_tile = jnp.where(seen, t_tile, NEG)
                s_tile = jnp.where(seen, s_tile, NEG)
            scores_t[span(c, n), :] = t_tile
            scores_s[span(c, n), :] = s_tile
            return (
                jnp.maximum(tops[0], jnp.max(eights(t_tile), axis=0)),
                jnp.maximum(tops[1], jnp.max(eights(s_tile), axis=0)),
            )

        def run(begin, stop, carry, body, n=1):
            return lax.fori_loop(0, (stop - begin) // n, lambda i, v: body(begin + n * i, v, n), carry)

        def run_all(begin, stop, carry, body):
            for n in (4, 2, 1):
                middle = stop - (stop - begin) % n
                carry = run(begin, middle, carry, body, n)
                begin = middle
            return carry

        from_tile = low // TILE
        plain_tile = jnp.minimum((high + TILE - 1) // TILE, t)
        tops = (jnp.full((8, TILE), NEG, F32), jnp.full((8, TILE), NEG, F32))
        tops = run_all(from_tile, plain_tile, tops, functools.partial(score, masked=True))
        tops = run_all(plain_tile, t, tops, functools.partial(score, masked=False))
        tops = score(t, tops, 1, True)
        top_t = jnp.max(tops[0], axis=0, keepdims=True)
        top_s = jnp.max(tops[1], axis=0, keepdims=True)

        def add(c, sums, n):
            sum_t, sum_s, cross = sums
            t_tile = scores_t[span(c, n), :]
            s_tile = scores_s[span(c, n), :]
            p = jnp.exp2(t_tile - top_t)
            q = jnp.exp2(s_tile - top_s)
            return (
                sum_t + jnp.sum(eights(p), axis=0),
                sum_s + jnp.sum(eights(q), axis=0),
                cross + jnp.sum(eights(p * (t_tile - s_tile)), axis=0),
            )

        zero = jnp.zeros((8, TILE), F32)
        sums = run_all(from_tile, t + 1, (zero, zero, zero), add)
        sum_t, sum_s, cross = (jnp.sum(v, axis=0, keepdims=True) for v in sums)
        lse_t = top_t * LN2 + jnp.log(sum_t)
        lse_s = top_s * LN2 + jnp.log(sum_s)
        row_kl = cross * LN2 / sum_t - lse_t + lse_s
        for k, lse in enumerate((lse_t, lse_s)):
            high_part = lse.astype(BF16).astype(F32)
            low_part = (lse - high_part).astype(BF16).astype(F32)
            out[2 * half + k:2 * half + k + 1, :] = (high_part + low_part) * LOG2E
        out[4 + half:5 + half, :] = row_kl


def grad_kernel(*refs):
    parts, packets, outs = refs[:12], refs[12:16], refs[16:20]
    rows, norms, row_norm, acc, mine = refs[20:]
    bounds = assemble(parts, rows)
    y, z, core = placed()
    m = z // 2
    kl = jnp.zeros((1, TILE), F32)
    for i, packet in enumerate(packets):
        for other in range(2):
            from_core = core if other == 0 else 1 - core
            from_r = (y ^ i) * 2 + from_core
            norms[from_r, 0:2, :] = packet[8 * other:8 * other + 2, :]
            norms[TILES - 1 - from_r, 0:2, :] = packet[8 * other + 2:8 * other + 4, :]
            kl = kl + packet[8 * other + 4:8 * other + 5, :] + packet[8 * other + 5:8 * other + 6, :]
    kl = kl[:, 0:128] + kl[:, 128:256]
    first = y * (2 * BLOCK) + core * ROWS
    last = first + 7 * ROWS - 1
    for b in range(4):
        sub = slice(b * ROWS, (b + 1) * ROWS)
        mine[sub, :] = rows[pl.ds(pl.multiple_of(first + 2 * b * ROWS, ROWS), ROWS), :]
        for k in range(2):
            line = norms[4 * y + b, k:k + 1, :]
            line = jnp.where(core == 0, line[:, 0:ROWS], line[:, ROWS:TILE])
            row_norm[k, sub] = jnp.transpose(jnp.broadcast_to(line, (ROWS, ROWS)))
    my_index = lax.broadcasted_iota(jnp.int32, (BLOCK, 1), 0)
    my_pos = first + my_index + (my_index // ROWS) * ROWS
    my_posf = my_pos.astype(F32)
    my_start = jnp.max(jnp.where(bounds <= my_posf, bounds, 0.0), axis=1, keepdims=True)
    my_end = jnp.min(jnp.where(bounds > my_posf, bounds, float(TOKENS)), axis=1, keepdims=True)
    my_start, my_end = my_start.astype(jnp.int32), my_end.astype(jnp.int32)
    firstf, lastf = first.astype(F32), last.astype(F32)
    start_low = start_of(bounds, firstf).astype(jnp.int32)
    start_high = start_of(bounds, lastf).astype(jnp.int32)
    end_low = end_of(bounds, firstf).astype(jnp.int32)
    end_high = end_of(bounds, lastf).astype(jnp.int32)
    acc[...] = jnp.zeros_like(acc)

    def columns(c, n):
        return pl.ds(pl.multiple_of(c * TILE, TILE), n * TILE)

    def step(c, n, kind, masked):
        width = n * TILE
        pupil = rows[columns(c, n), TDIM:WIDE]
        t_tile = nt_dot(mine[:, 0:TDIM], rows[columns(c, n), 0:TDIM]) * KT
        s_tile = nt_dot(mine[:, TDIM:WIDE], pupil) * KS
        own_norm = [jnp.concatenate([row_norm[k]] * (2 * n), axis=1) for k in range(2)]
        their_norm = [jnp.concatenate([norms[c + q, k:k + 1, :] for q in range(n)], axis=1) for k in range(2)]
        pos = c * TILE + lax.broadcasted_iota(jnp.int32, (BLOCK, width), 1)
        if kind == "below":
            norm_t, norm_s = own_norm
        elif kind == "above":
            norm_t, norm_s = their_norm
        else:
            own = pos <= my_pos
            norm_t, norm_s = (jnp.where(own, own_norm[k], their_norm[k]) for k in range(2))
        weight = jnp.exp2(s_tile - norm_s) - jnp.exp2(t_tile - norm_t)
        if kind == "diagonal":
            weight = jnp.where(pos == my_pos, 2.0 * weight, weight)
        if masked:
            weight = jnp.where((pos >= my_start) & (pos < my_end), weight, 0.0)
        acc[...] += jnp.dot(weight.astype(BF16), pupil, preferred_element_type=F32)

    def run(begin, stop, kind, masked, n=1):
        def body(i, unused):
            step(begin + n * i, n, kind, masked)
            return unused

        lax.fori_loop(0, (stop - begin) // n, body, 0)

    wide = UNROLL * TILE
    diag = 4 * y
    plain = jnp.minimum((start_high + wide - 1) // wide * UNROLL, diag)
    run(start_low // wide * UNROLL, plain, "below", True, UNROLL)
    run(plain, diag, "below", False, UNROLL)
    run(diag, diag + 4, "diagonal", True, UNROLL)
    plain = jnp.maximum(end_low // wide * UNROLL, diag + 4)
    run(diag + 4, plain, "above", False, UNROLL)
    run(plain, (end_high + wide - 1) // wide * UNROLL, "above", True, UNROLL)
    for b in range(4):
        for j in range(4):

            @pl.when((m - j + 4) % 4 == b)
            def _():
                outs[j][0:ROWS, :] = acc[b * ROWS:(b + 1) * ROWS, :].astype(BF16)

    high_part = kl.astype(BF16).astype(F32)
    mid_part = (kl - high_part).astype(BF16).astype(F32)
    low_part = (kl - high_part - mid_part).astype(BF16).astype(F32)
    line = lax.broadcasted_iota(jnp.int32, (16, 128), 0)
    tail = jnp.where(line == 0, high_part, jnp.where(line == 1, mid_part, jnp.where(line == 2, low_part, 0.0)))
    for j in range(4):
        outs[j][ROWS:ROWS + 16, :] = tail.astype(BF16)


def finish_kernel(g0, g1, g2, g3, grad_q, grad_k, held):
    b = placed()[1] // 2
    for j, got in enumerate((g0, g1, g2, g3)):
        held[(b + j) % 4] = got[0:ROWS, :]
    for m in range(4):
        out = grad_q if m < 2 else grad_k
        h = m % 2
        out[:, h * HDIM:(h + 1) * HDIM] = held[m]


def call_norm(parts):
    return pl.pallas_call(
        norm_kernel,
        out_shape=jax.ShapeDtypeStruct((8, TILE), F32),
        in_specs=[ALL] * 12,
        out_specs=ALL,
        scratch_shapes=[
            pltpu.VMEM((TOKENS, WIDE), BF16),
            pltpu.VMEM((TOKENS, TILE), F32),
            pltpu.VMEM((TOKENS, TILE), F32),
        ],
        compiler_params=params(),
    )(*parts)


def call_grad(parts, packets):
    return pl.pallas_call(
        grad_kernel,
        out_shape=[jax.ShapeDtypeStruct((ROWS + 16, HDIM), BF16)] * 4,
        in_specs=[ALL] * 16,
        out_specs=[ALL] * 4,
        scratch_shapes=[
            pltpu.VMEM((TOKENS, WIDE), BF16),
            pltpu.VMEM((TILES, 8, TILE), F32),
            pltpu.VMEM((2, BLOCK, 128), F32),
            pltpu.VMEM((BLOCK, HDIM), F32),
            pltpu.VMEM((BLOCK, WIDE), BF16),
        ],
        compiler_params=params(),
    )(*parts, *packets)


def per_device(teacher_query, teacher_key, student_query, student_key, doc_ids):
    block = jax.ShapeDtypeStruct((ROWS + 16, WIDE), BF16)
    sends = pl.pallas_call(
        send_kernel,
        out_shape=[block] * 4,
        in_specs=[ANY] * 5,
        out_specs=[ALL] * 4,
        scratch_shapes=[
            pltpu.VMEM((4, ROWS, WIDE), BF16),
            pltpu.VMEM((1, ROWS), jnp.int32),
            pltpu.SemaphoreType.DMA((9,)),
        ],
        compiler_params=params(60 * 1024 * 1024),
    )(teacher_query, teacher_key, student_query, student_key, doc_ids.reshape(1, ROWS))
    gots = [lax.ppermute(sends[j], AXES, spread_pairs(j)) for j in ORDER]
    piece = jax.ShapeDtypeStruct((PIECE, WIDE), BF16)
    own_a = pl.pallas_call(
        pack_kernel,
        out_shape=piece,
        in_specs=[ALL] * 2,
        out_specs=ALL,
        compiler_params=params(),
        cost_estimate=pl.CostEstimate(
            flops=PACK_FLOPS, bytes_accessed=4 * PIECE * WIDE, transcendentals=0
        ),
    )(*gots[0:2])
    own_b, own = pl.pallas_call(
        pack_both_kernel,
        out_shape=[piece, jax.ShapeDtypeStruct((2 * PIECE, WIDE), BF16)],
        in_specs=[ALL] * 3,
        out_specs=[ALL] * 2,
        compiler_params=params(),
    )(own_a, *gots[2:4])
    near_a, near_b = (lax.ppermute(mine, AXES, near_pairs(1)) for mine in (own_a, own_b))
    far_a, far_b = (lax.ppermute(mine, AXES, near_pairs(-1)) for mine in (own_a, own_b))
    over_a, over_b = (lax.ppermute(near, AXES, near_pairs(1)) for near in (near_a, near_b))
    parts = [own, near_a, far_a, over_a, group([near_b, far_b]), over_b]
    parts += [lax.ppermute(part, AXES, CORE_PAIRS) for part in parts]
    packet = call_norm(parts)
    both = jnp.concatenate([packet, lax.ppermute(packet, AXES, CORE_PAIRS)])
    others = {step: lax.ppermute(both, AXES, mirror_pairs(step)) for step in (3, 1, 2)}
    packets = [both] + [others[step] for step in (1, 2, 3)]
    grads = call_grad(parts, packets)
    backs = {j: lax.ppermute(grads[j], AXES, collect_pairs(j)) for j in (2, 3, 1, 0)}
    backs = [backs[j] for j in range(4)]
    kl = sum(back[ROWS:ROWS + 16].astype(F32) for back in backs)
    kl = jnp.sum(kl.reshape(2, 8, HDIM), axis=0)
    kl = kl + lax.ppermute(kl, AXES, CORE_PAIRS)
    kl = kl + sum(lax.ppermute(kl, AXES, x_pairs(bits)) for bits in (1, 2, 3))
    kl_loss = jnp.sum(kl) / (2.0 * TOKENS * 16)
    half_grad = jax.ShapeDtypeStruct((ROWS, 2 * HDIM), BF16)
    grad_query, grad_key = pl.pallas_call(
        finish_kernel,
        out_shape=[half_grad, half_grad],
        in_specs=[ALL] * 4,
        out_specs=[ALL] * 2,
        scratch_shapes=[pltpu.VMEM((4, ROWS, HDIM), BF16)],
        compiler_params=params(),
    )(*backs)
    return (kl_loss, grad_query, grad_key)


def solution(mesh):
    in_specs = (P("seq", "head"), P("seq", "head"), P("seq", "head"), P("seq", "head"), P("seq"))
    out_specs = (P(), P("seq", "head"), P("seq", "head"))
    return jax.shard_map(
        per_device, mesh=mesh, in_specs=in_specs, out_specs=out_specs, check_vma=False
    )
```
